512 devices in a mesh: row: 64 (over y_lo, z, core), col: 8 (over x, y_hi).
Axes of the slice: x: 4, y: 4 (y_hi: 2, y_lo: 2; y = y_hi * 2 + y_lo), z: 16, core: 2. Of those that a mesh axis runs over, the one named last changes fastest.
Arguments:
- x_tiles: bfloat16 [192, 32, 128, 128], P('row', 'col'), may hold values from -0.59765625 to 0.59765625
- tile_cols: int32 [192, 32], P('row', 'col'), may hold values from 0 to 191, as said below
- tile_counts: int32 [192, 8], P('row', 'col'), may hold values from 1 to 4
Outputs:
- product: bfloat16 [192, 32, 128, 128], P('row', 'col')
The draws below stay inside these ranges and needn't reach their ends.
Inputs may be any that keep to these rules, and one draw needn't show every extreme that they name: `tile_cols`: in block row i the slots p * 4 to (p + 1) * 4 - 1 hold 4 distinct block columns of panel p, each of the form p * 24 + ((i + d) mod 24) with -2 <= d <= 2.
All inputs are finite; a program needn't handle non-finite values.
Results may differ from the reference program's by a relative error of at most 0.001.
Values may be sent and summed in bfloat16 or wider, within the bound.
No kernel may reach another device: no remote copies, remote signals or barrier semaphores. Data moves between devices by JAX's collectives and lax.ppermute only.
A program may use at most 128 MiB of HBM per device.

```python
import jax
import jax.numpy as jnp
from jax import lax

TILE = 128
PANELS = 8
PS = 4
HALF = 2
NB = 192
SLOTS = 32


def draw_tile_cols(key, part):
    key = jax.random.fold_in(key, 11)
    width = NB // PANELS
    reach = 2 * HALF + 1
    scores = jax.random.randint(key, (NB, PANELS, reach), 0, 1 << 20)
    scores = scores * reach + jnp.arange(reach, dtype=jnp.int32)[None, None, :]
    order = jnp.argsort(scores, axis=-1)[..., :PS].astype(jnp.int32)
    shifted = order - HALF
    rows = jnp.arange(NB, dtype=jnp.int32)[:, None, None]
    inside = (rows % width + shifted + width) % width
    offsets = (jnp.arange(PANELS, dtype=jnp.int32) * width)[None, :, None]
    return (inside + offsets).reshape(NB, PANELS * PS).astype(jnp.int32)


def draw_tile_counts(key, part):
    key = jax.random.fold_in(key, 23)
    counts = jax.random.randint(key, (NB, PANELS), 1, PS + 1)
    rows = jnp.arange(NB, dtype=jnp.int32)[:, None]
    panels = jnp.arange(PANELS, dtype=jnp.int32)[None, :]
    marker = (rows * 5 + panels * 3) % 7
    counts = jnp.where(marker == 0, PS, counts)
    counts = jnp.where(marker == 3, 1, counts)
    return counts.astype(jnp.int32)


def block_scale(key, shape, cuts, least, largest):
    loudness, own = 1.0, jax.random.fold_in(key, 6)
    for dim, parts in cuts:
        heights = jnp.exp(jax.random.uniform(jax.random.fold_in(own, dim), (parts,), jnp.float32, least / len(cuts), largest / len(cuts)))
        loudness = loudness * jnp.repeat(heights, shape[dim] // parts).reshape([-1 if axis == dim else 1 for axis in range(len(shape))])
    return loudness


def centred(own_key, extent, spread, limit, pieces=(), held_as=jnp.bfloat16):
    level = block_scale(own_key, extent, pieces, -0.22, 0.18) if pieces else 1.0
    entries = jax.random.normal(own_key, extent, jnp.float32) * spread * level
    return jnp.minimum(jnp.maximum(entries, -limit), limit).astype(held_as)


def setup_inputs(seed: int = 0) -> dict:
    arg_keys = jax.random.split(jax.random.key(seed), 4)
    return {
        "x_tiles": centred(arg_keys[0], (NB, SLOTS, TILE, TILE), 0.1, 0.59765625, ((0, 64), (1, 8))),
        "tile_cols": draw_tile_cols(jax.random.fold_in(arg_keys[3], 71), 0),
        "tile_counts": draw_tile_counts(jax.random.fold_in(arg_keys[3], 71), 0),
    }


def slot_live(tile_cols, tile_counts):
    repeated = jnp.repeat(tile_counts, PS, axis=1)
    position = lax.broadcasted_iota(jnp.int32, tile_cols.shape, 1) % PS
    return position < repeated


def reference(x_tiles, tile_cols, tile_counts):
    live = slot_live(tile_cols, tile_counts)
    masked = jnp.where(live[:, :, None, None], x_tiles, jnp.zeros((), x_tiles.dtype))
    keyed = jnp.where(live, tile_cols, -1).astype(jnp.int32)

    def one_row(index):
        left = masked[index].astype(jnp.float32)
        left_cols = tile_cols[index]
        right = masked[left_cols].astype(jnp.float32)
        right_keyed = keyed[left_cols]
        hits = (right_keyed[:, :, None] == left_cols[None, None, :]).astype(jnp.float32)
        placed = jnp.einsum("tus,tuxy->tsxy", hits, right)
        summed = jnp.einsum("txy,tsyz->sxz", left, placed)
        return jnp.where(live[index][:, None, None], summed, 0.0).astype(jnp.bfloat16)

    return lax.map(one_row, jnp.arange(NB, dtype=jnp.int32))
```

```python
import functools

import jax
import jax.numpy as jnp
from jax import lax
from jax.experimental import pallas as pl
from jax.experimental.pallas import tpu as pltpu
from jax.sharding import PartitionSpec as P

BF16, F32, I32 = jnp.bfloat16, jnp.float32, jnp.int32
T = 128
LIMIT = 48 << 20
BLOCK = 12 * T + 16
HEAD, TAIL = T, T + 16
PIECE = 3 * (HEAD + TAIL)
ANY = pl.BlockSpec(memory_space=pl.ANY)
VMEM = pl.BlockSpec(memory_space=pltpu.VMEM)
SMEM = pl.BlockSpec(memory_space=pltpu.SMEM)


def routes(move):
    pairs = []
    for row in range(64):
        for col in range(8):
            a, z, k, x, h = move(row // 32, row // 2 % 16, row % 2, col // 2, col % 2)
            pairs.append((row * 8 + col, (a * 32 + z % 16 * 2 + k) * 8 + x % 4 * 2 + h))
    return pairs


def along_z(n):
    return routes(lambda a, z, k, x, h: (a, z + n, k, x, h))


def along_x(n):
    return routes(lambda a, z, k, x, h: (a, z, k, x + n, h))


def along_y(n):
    def move(a, z, k, x, h):
        y = (2 * h + a + n) % 4
        return y % 2, z, k, x, y // 2

    return routes(move)


CORE = routes(lambda a, z, k, x, h: (a, z, 1 - k, x, h))
HALO = routes(lambda a, z, k, x, h: (a, z + 2 * k - 1, 1 - k, x, h))
PLANE = routes(lambda a, z, k, x, h: (1 - a, z, k, x, h))


def send(block, pairs):
    return lax.ppermute(block, ("row", "col"), pairs)


def params():
    return pltpu.CompilerParams(vmem_limit_bytes=LIMIT)


def cost(flops, moved):
    return pl.CostEstimate(flops=flops, bytes_accessed=moved, transcendentals=0)


def lanes():
    return lax.broadcasted_iota(I32, (1, T), 1)


def turned(v):
    return pltpu.roll(v, T // 2, 1)


def pack_kernel(place, cols, counts, x, a_out, b0_out, b1_out, k_out):
    row = lax.broadcasted_iota(I32, (16, T), 0)
    left = lax.broadcasted_iota(I32, (16, T), 1) < T // 2
    plain = jnp.full((16, T), 9, I32)
    paired = jnp.full((16, T), 9, I32)
    for r in range(3):
        keys = []
        for t in range(4):
            away = (cols[r, t] - (place[0] * 3 + r) + 240) % 24
            away = jnp.where(away > 12, away - 24, away)
            keys.append(jnp.where(t < counts[r, 0], away, 9))
            plain = jnp.where(row == r * 4 + t, keys[t], plain)
        for m in range(2):
            first, second = keys[2 * m], keys[2 * m + 1]
            paired = jnp.where(row == r * 4 + 2 * m, jnp.where(left, first, second), paired)
            paired = jnp.where(row == r * 4 + 2 * m + 1, jnp.where(left, second, first), paired)
    a_out[12 * T :, :] = plain.astype(F32).astype(BF16)
    paired = paired.astype(F32)
    k_out[...] = paired.astype(BF16)
    here = lanes() < T // 2
    for r in range(3):
        tail = 3 * HEAD + r * TAIL
        keyed = jnp.concatenate([paired[4 * r : 4 * r + 4], jnp.full((12, T), 9.0, F32)], axis=0)
        keyed = keyed.astype(BF16)
        b0_out[tail + T : tail + TAIL, :] = keyed
        b1_out[tail + T : tail + TAIL, :] = keyed
        for m in range(2):
            at = r * HEAD if m == 0 else tail
            even = x[r, 2 * m]
            odd = x[r, 2 * m + 1]
            a_out[(4 * r + 2 * m) * T : (4 * r + 2 * m + 1) * T, :] = even
            a_out[(4 * r + 2 * m + 1) * T : (4 * r + 2 * m + 2) * T, :] = odd
            even, odd = even.astype(F32), odd.astype(F32)
            b0_out[at : at + T, :] = jnp.where(here, even, turned(odd)).astype(BF16)
            b1_out[at : at + T, :] = jnp.where(here, turned(even), odd).astype(BF16)


def pack(place, cols, counts, x):
    shapes = ((BLOCK, T), (PIECE, T), (PIECE, T), (16, T))
    return pl.pallas_call(
        pack_kernel,
        out_shape=[jax.ShapeDtypeStruct(s, BF16) for s in shapes],
        in_specs=[SMEM, SMEM, SMEM, VMEM],
        out_specs=[VMEM] * 4,
        compiler_params=params(),
        cost_estimate=cost(1 << 20, 6 << 20),
        name="pack",
    )(place, cols, counts, x)


def run_all(copies):
    for copy in copies:
        copy.start()
    for copy in copies:
        copy.wait()


def sort_kernel(place, own, g1, g2, g3, keys, same, other, sem):
    a, x = place[1], place[4]
    last = pltpu.make_async_copy(keys, other.at[pl.ds(2 * BLOCK, 16)], sem.at[4])
    last.start()
    copies = []
    for k, source in enumerate((own, g1, g2, g3)):
        panel = (x - k + 4) % 4
        at = pl.multiple_of(panel % 2 * BLOCK, 16)
        to_same = pltpu.make_async_copy(source, same.at[pl.ds(at, BLOCK)], sem.at[k])
        to_other = pltpu.make_async_copy(source, other.at[pl.ds(at, BLOCK)], sem.at[k])
        pl.when(panel // 2 == a)(to_same.start)
        pl.when(panel // 2 != a)(to_other.start)
        copies.append(to_same)
    for copy in copies:
        copy.wait()
    last.wait()


def sort_panels(place, own, g1, g2, g3, keys):
    return pl.pallas_call(
        sort_kernel,
        out_shape=[
            jax.ShapeDtypeStruct((2 * BLOCK, T), BF16),
            jax.ShapeDtypeStruct((2 * BLOCK + 16, T), BF16),
        ],
        in_specs=[SMEM] + [ANY] * 5,
        out_specs=[ANY] * 2,
        scratch_shapes=[pltpu.SemaphoreType.DMA((5,))],
        compiler_params=params(),
        cost_estimate=cost(0, 4 << 20),
        name="sort_panels",
    )(place, own, g1, g2, g3, keys)


def left_kernel(place, same, r1, rm, r2, out, partner, held, sem):
    a, h = place[1], place[5]
    copies = []
    near = jnp.where(a == 1, h, 1 - h)
    for q, (source, half) in enumerate(((same, h), (r2, 1 - h), (r1, near), (rm, 1 - near))):
        for e in range(2):
            copies.append(
                pltpu.make_async_copy(
                    source.at[pl.ds(e * BLOCK, BLOCK)],
                    held.at[q // 2 * 4 + 2 * e + half],
                    sem.at[2 * q + e],
                )
            )
    for copy in copies:
        copy.start()
    from_r1 = pltpu.make_async_copy(r1.at[pl.ds(2 * BLOCK, 16)], partner, sem.at[8])
    from_rm = pltpu.make_async_copy(rm.at[pl.ds(2 * BLOCK, 16)], partner, sem.at[8])
    pl.when(a == 1)(from_r1.start)
    pl.when(a == 0)(from_rm.start)
    for copy in copies:
        copy.wait()
    from_r1.wait()

    def one(q, carry):
        low = pl.multiple_of(q // 4 * T, T)
        keys = held[q, 12 * T :, :].astype(F32)
        for i in range(3):
            tiles = [held[q, (4 * i + t) * T : (4 * i + t + 1) * T, :].astype(F32) for t in range(4)]
            for d in range(5):
                parts = [
                    tiles[t] * jnp.where(keys[4 * i + t : 4 * i + t + 1] == float(d - 2), 1.0, 0.0)
                    for t in range(4)
                ]
                block = (parts[0] + parts[1]) + (parts[2] + parts[3])
                out[i, q % 4, pl.ds(low, T), d * T : (d + 1) * T] = block.astype(BF16)
        return carry

    lax.fori_loop(0, 8, one, 0)


def left_panels(place, same, r1, rm, r2):
    return pl.pallas_call(
        left_kernel,
        out_shape=[
            jax.ShapeDtypeStruct((3, 4, 2 * T, 5 * T), BF16),
            jax.ShapeDtypeStruct((16, T), BF16),
        ],
        in_specs=[SMEM] + [ANY] * 4,
        out_specs=[VMEM, VMEM],
        scratch_shapes=[pltpu.VMEM((8, BLOCK, T), BF16), pltpu.SemaphoreType.DMA((9,))],
        compiler_params=params(),
        cost_estimate=cost(20 << 20, 8 << 20),
        name="left_panels",
    )(place, same, r1, rm, r2)


def edge_kernel(place, own, up, down, far_head, far_tail, to_core, to_halo, sem):
    b, core = place[2], place[3]
    copies = []
    for n, (out, start) in enumerate(((to_core, 1 - core), (to_halo, core))):
        for k, (source, panel) in enumerate(((own, b), (up, (b + 3) % 4), (down, (b + 1) % 4), (None, (b + 2) % 4))):
            head, tail = (source, source) if source is not None else (far_head, far_tail)
            base = 3 * HEAD if source is not None else 0
            copies.append(
                pltpu.make_async_copy(
                    head.at[pl.ds(pl.multiple_of(start * HEAD, 16), 2 * HEAD)],
                    out.at[panel, pl.ds(0, 2 * HEAD)],
                    sem.at[8 * n + 2 * k],
                )
            )
            copies.append(
                pltpu.make_async_copy(
                    tail.at[pl.ds(pl.multiple_of(base + start * TAIL, 16), 2 * TAIL)],
                    out.at[panel, pl.ds(2 * HEAD, 2 * TAIL)],
                    sem.at[8 * n + 2 * k + 1],
                )
            )
    run_all(copies)


def edges(place, own, up, down, far_head, far_tail):
    shape = jax.ShapeDtypeStruct((4, 2 * (HEAD + TAIL), T), BF16)
    return pl.pallas_call(
        edge_kernel,
        out_shape=[shape, shape],
        in_specs=[SMEM] + [ANY] * 5,
        out_specs=[ANY] * 2,
        scratch_shapes=[pltpu.SemaphoreType.DMA((16,))],
        compiler_params=params(),
        cost_estimate=cost(0, 4 << 20),
        name="edges",
    )(place, own, up, down, far_head, far_tail)


def multiply_kernel(
    place, own, up, down, far_head, far_tail, from_core, from_halo, left, mine, partner,
    keep, give, heads, tails, right, sem,
):
    b, core = place[2], place[3]
    copies = []
    for k, (source, panel) in enumerate(((own, b), (up, (b + 3) % 4), (down, (b + 1) % 4), (None, (b + 2) % 4))):
        head = far_head if source is None else source.at[pl.ds(0, 3 * HEAD)]
        tail = far_tail if source is None else source.at[pl.ds(3 * HEAD, 3 * TAIL)]
        copies.append(pltpu.make_async_copy(head, heads.at[panel, pl.ds(2 * HEAD, 3 * HEAD)], sem.at[2 * k]))
        copies.append(pltpu.make_async_copy(tail, tails.at[panel, pl.ds(2 * TAIL, 3 * TAIL)], sem.at[2 * k + 1]))
    for k, (source, slot) in enumerate(((from_core, 5 * (1 - core)), (from_halo, 5 * core))):
        copies.append(
            pltpu.make_async_copy(
                source.at[:, pl.ds(0, 2 * HEAD)],
                heads.at[:, pl.ds(pl.multiple_of(slot * HEAD, 16), 2 * HEAD)],
                sem.at[8 + 2 * k],
            )
        )
        copies.append(
            pltpu.make_async_copy(
                source.at[:, pl.ds(2 * HEAD, 2 * TAIL)],
                tails.at[:, pl.ds(pl.multiple_of(slot * TAIL, 16), 2 * TAIL)],
                sem.at[9 + 2 * k],
            )
        )
    run_all(copies)
    half = (lanes() >= T // 2).astype(F32)
    zero = jnp.zeros((T, T), BF16)
    sums = [None] * 3
    for p in range(4):
        for k in range(7):
            keys = tails[p, k * TAIL + T : (k + 1) * TAIL, :].astype(F32) + float(k)
            v0 = heads[p, k * HEAD : (k + 1) * HEAD, :].astype(F32)
            v1 = tails[p, k * TAIL : k * TAIL + T, :].astype(F32)
            w0, w1 = turned(v0), turned(v1)
            for w in range(4):
                into = (p % 2, slice(k * T, (k + 1) * T), slice(w * T, (w + 1) * T))
                if 2 * w + 1 < k - 2 or 2 * w > k + 2:
                    right[into] = zero
                    continue
                target = half + float(2 * w)
                pick = [jnp.where(keys[n : n + 1] == target, 1.0, 0.0) for n in range(4)]
                block = (v0 * pick[0] + w0 * pick[1]) + (v1 * pick[2] + w1 * pick[3])
                right[into] = block.astype(BF16)
        for i in range(3):
            first = i // 2 * T
            part = jnp.dot(
                left[i, p],
                right[p % 2, i * T : (i + 5) * T, first : first + 3 * T],
                preferred_element_type=F32,
            )
            sums[i] = part if sums[i] is None else sums[i] + part
    for i in range(3):
        for side, (out, source) in enumerate(((keep, mine), (give, partner))):
            keys = source[...].astype(F32)[4 * i : 4 * i + 4] + float(i + 2)
            for m in range(2):
                total = None
                for w in range(3):
                    v = sums[i][side * T : (side + 1) * T, w * T : (w + 1) * T]
                    target = half + float(2 * (w + i // 2))
                    swap = (1.0 - half) + float(2 * (w + i // 2))
                    key = keys[2 * m : 2 * m + 1]
                    part = v * jnp.where(key == target, 1.0, 0.0)
                    part = part + turned(v) * jnp.where(key == swap, 1.0, 0.0)
                    total = part if total is None else total + part
                out[i, m] = total


def multiply(place, pieces, received, left, mine, partner):
    shape = jax.ShapeDtypeStruct((3, 2, T, T), F32)
    return pl.pallas_call(
        multiply_kernel,
        out_shape=[shape, shape],
        in_specs=[SMEM] + [ANY] * 7 + [VMEM] * 3,
        out_specs=[VMEM, VMEM],
        scratch_shapes=[
            pltpu.VMEM((4, 7 * HEAD, T), BF16),
            pltpu.VMEM((4, 7 * TAIL, T), BF16),
            pltpu.VMEM((2, 7 * T, 4 * T), BF16),
            pltpu.SemaphoreType.DMA((12,)),
        ],
        compiler_params=params(),
        cost_estimate=cost(3 << 30, 10 << 20),
        name="multiply",
    )(place, *pieces, *received, left, mine, partner)


def finish_kernel(own0, got0, own1, got1, out):
    here = lanes() < T // 2
    for i in range(3):
        for m in range(2):
            low = own0[i, m] + got0[i, m]
            high = own1[i, m] + got1[i, m]
            out[i, 2 * m] = jnp.where(here, low, turned(high)).astype(BF16)
            out[i, 2 * m + 1] = jnp.where(here, turned(low), high).astype(BF16)


def finish(own0, got0, own1, got1):
    return pl.pallas_call(
        finish_kernel,
        out_shape=jax.ShapeDtypeStruct((3, 4, T, T), BF16),
        in_specs=[VMEM] * 4,
        out_specs=VMEM,
        compiler_params=params(),
        cost_estimate=cost(1 << 20, 2 << 20),
        name="finish",
    )(own0, got0, own1, got1)


def after(value, *others):
    return lax.optimization_barrier((value,) + others)[0]


def body(x_tiles, tile_cols, tile_counts):
    row, col = lax.axis_index("row"), lax.axis_index("col")
    place = jnp.stack([row, row // 32, row // 8 % 4, row % 2, col // 2, col % 2]).astype(I32)
    block, piece0, piece1, keys = pack(place, tile_cols, tile_counts, x_tiles)
    own = (piece0, piece1)
    up = [None, None]
    down = [None, None]
    far_head = [None, None]
    far_tail = [None, None]
    for h in range(2):
        up[h], down[h] = send(own[h], along_z(4)), send(own[h], along_z(-4))
    g1, g3, g2 = send(block, along_x(1)), send(block, along_x(-1)), send(block, along_x(2))
    for h in range(2):
        far_head[h] = send(up[h][: 3 * HEAD], along_z(4))
        far_tail[h] = send(down[h][3 * HEAD :], along_z(-4))
    same, other = sort_panels(place, block, g1, g2, g3, keys)
    r1, rm, r2 = send(other, along_y(1)), send(other, along_y(-1)), send(same, along_y(2))
    left, partner = left_panels(place, same, r1, rm, r2)
    kept, got = [], []
    for h in range(2):
        pieces = (own[h], up[h], down[h], far_head[h], far_tail[h])
        to_core, to_halo = edges(place, *pieces)
        received = (send(to_core, CORE), send(to_halo, HALO))
        keep, give = multiply(place, pieces, received, left, keys, partner)
        kept.append(keep)
        got.append(send(give, PLANE))
    return finish(kept[0], got[0], kept[1], got[1])


def solution(mesh):
    placed = (P("row", "col", None, None), P("row", "col"), P("row", "col"))
    return jax.shard_map(
        body, mesh=mesh, in_specs=placed, out_specs=P("row", "col", None, None), check_vma=False
    )
```

```python
import functools

import jax
import jax.numpy as jnp
from jax import lax
from jax.experimental import pallas as pl
from jax.experimental.pallas import tpu as pltpu
from jax.sharding import PartitionSpec as P

BF16, F32, I32 = jnp.bfloat16, jnp.float32, jnp.int32
T = 128
EDGE = (0, 0)
MULT = (3 << 30, 3 << 30)
LEFT = 5700000000
SORT = 0
LIMIT = 48 << 20
BLOCK = 12 * T + 16
HEAD, TAIL = T, T + 16
PIECE = 3 * (HEAD + TAIL)
ANY = pl.BlockSpec(memory_space=pl.ANY)
VMEM = pl.BlockSpec(memory_space=pltpu.VMEM)
SMEM = pl.BlockSpec(memory_space=pltpu.SMEM)


def routes(move):
    pairs = []
    for row in range(64):
        for col in range(8):
            a, z, k, x, h = move(row // 32, row // 2 % 16, row % 2, col // 2, col % 2)
            pairs.append((row * 8 + col, (a * 32 + z % 16 * 2 + k) * 8 + x % 4 * 2 + h))
    return pairs


def along_z(n):
    return routes(lambda a, z, k, x, h: (a, z + n, k, x, h))


def along_x(n):
    return routes(lambda a, z, k, x, h: (a, z, k, x + n, h))


def along_y(n):
    def move(a, z, k, x, h):
        y = (2 * h + a + n) % 4
        return y % 2, z, k, x, y // 2

    return routes(move)


CORE = routes(lambda a, z, k, x, h: (a, z, 1 - k, x, h))
HALO = routes(lambda a, z, k, x, h: (a, z + 2 * k - 1, 1 - k, x, h))
PLANE = routes(lambda a, z, k, x, h: (1 - a, z, k, x, h))


def send(block, pairs):
    return lax.ppermute(block, ("row", "col"), pairs)


def params():
    return pltpu.CompilerParams(vmem_limit_bytes=LIMIT)


def cost(flops, moved):
    return pl.CostEstimate(flops=flops, bytes_accessed=moved, transcendentals=0)


def lanes():
    return lax.broadcasted_iota(I32, (1, T), 1)


def flipped(v):
    return pltpu.roll(v, T // 2, 1)


def chosen(keys, target):
    return jnp.where(keys == target, 1.0, 0.0).astype(BF16)


def turned(v):
    return pltpu.roll(v, T // 2, 1)


def pack_kernel(place, cols_in, counts_in, x_in, a_out, b_out, k_out, cols, counts, x, sem):
    run_all(
        [
            pltpu.make_async_copy(cols_in, cols, sem.at[0]),
            pltpu.make_async_copy(counts_in, counts, sem.at[1]),
            pltpu.make_async_copy(x_in, x, sem.at[2]),
        ]
    )
    row = lax.broadcasted_iota(I32, (16, T), 0)
    left = lax.broadcasted_iota(I32, (16, T), 1) < T // 2
    plain = jnp.full((16, T), 9, I32)
    paired = jnp.full((16, T), 9, I32)
    for r in range(3):
        keys = []
        for t in range(4):
            away = (cols[r, t] - (place[0] * 3 + r) + 240) % 24
            away = jnp.where(away > 12, away - 24, away)
            keys.append(jnp.where(t < counts[0, r], away, 9))
            plain = jnp.where(row == r * 4 + t, keys[t], plain)
        for m in range(2):
            first, second = keys[2 * m], keys[2 * m + 1]
            paired = jnp.where(row == r * 4 + 2 * m, jnp.where(left, first, second), paired)
            paired = jnp.where(row == r * 4 + 2 * m + 1, jnp.where(left, second, first), paired)
    a_out[12 * T :, :] = plain.astype(F32).astype(BF16)
    paired = paired.astype(F32)
    k_out[...] = paired.astype(BF16)
    here = lanes() < T // 2
    for r in range(3):
        tail = 3 * HEAD + r * TAIL
        keyed = jnp.concatenate([paired[4 * r : 4 * r + 4], jnp.full((12, T), 9.0, F32)], axis=0)
        keyed = keyed.astype(BF16)
        b_out[tail + T : tail + TAIL, :] = keyed
        b_out[PIECE + tail + T : PIECE + tail + TAIL, :] = keyed
        for m in range(2):
            at = r * HEAD if m == 0 else tail
            even = x[r, 2 * m]
            odd = x[r, 2 * m + 1]
            a_out[(4 * r + 2 * m) * T : (4 * r + 2 * m + 1) * T, :] = even
            a_out[(4 * r + 2 * m + 1) * T : (4 * r + 2 * m + 2) * T, :] = odd
            even, odd = even.astype(F32), odd.astype(F32)
            b_out[at : at + T, :] = jnp.where(here, even, turned(odd)).astype(BF16)
            b_out[PIECE + at : PIECE + at + T, :] = jnp.where(here, turned(even), odd).astype(BF16)


def pack(place, cols, counts, x):
    shapes = ((BLOCK, T), (2 * PIECE, T), (16, T))
    return pl.pallas_call(
        pack_kernel,
        out_shape=[jax.ShapeDtypeStruct(s, BF16) for s in shapes],
        in_specs=[SMEM, ANY, ANY, ANY],
        out_specs=[VMEM] * 3,
        scratch_shapes=[
            pltpu.SMEM((3, 4), I32),
            pltpu.SMEM((1, 3), I32),
            pltpu.VMEM((3, 4, T, T), BF16),
            pltpu.SemaphoreType.DMA((3,)),
        ],
        compiler_params=params(),
        cost_estimate=cost(1 << 20, 6 << 20),
        name="pack",
    )(place, cols, counts.T, x)


def run_all(copies):
    for copy in copies:
        copy.start()
    for copy in copies:
        copy.wait()


def sort_kernel(place, own, g1, g2, g3, keys, same, other, sem):
    a, x = place[1], place[4]
    last = pltpu.make_async_copy(keys, other.at[pl.ds(2 * BLOCK, 16)], sem.at[4])
    last.start()
    copies = []
    for k, source in enumerate((own, g1, g2, g3)):
        panel = (x - k + 4) % 4
        at = pl.multiple_of(panel % 2 * BLOCK, 16)
        to_same = pltpu.make_async_copy(source, same.at[pl.ds(at, BLOCK)], sem.at[k])
        to_other = pltpu.make_async_copy(source, other.at[pl.ds(at, BLOCK)], sem.at[k])
        pl.when(panel // 2 == a)(to_same.start)
        pl.when(panel // 2 != a)(to_other.start)
        copies.append(to_same)
    for copy in copies:
        copy.wait()
    last.wait()


def sort_panels(place, own, g1, g2, g3, keys):
    return pl.pallas_call(
        sort_kernel,
        out_shape=[
            jax.ShapeDtypeStruct((2 * BLOCK, T), BF16),
            jax.ShapeDtypeStruct((2 * BLOCK + 16, T), BF16),
        ],
        in_specs=[SMEM] + [ANY] * 5,
        out_specs=[ANY] * 2,
        scratch_shapes=[pltpu.SemaphoreType.DMA((5,))],
        compiler_params=params(),
        cost_estimate=cost(SORT, 4 << 20),
        name="sort_panels",
    )(place, own, g1, g2, g3, keys)


def left_kernel(place, same, r1, rm, r2, out, partner, held, sem):
    a, h = place[1], place[5]
    copies = []
    near = jnp.where(a == 1, h, 1 - h)
    for q, (source, half) in enumerate(((same, h), (r2, 1 - h), (r1, near), (rm, 1 - near))):
        for e in range(2):
            copies.append(
                pltpu.make_async_copy(
                    source.at[pl.ds(e * BLOCK, BLOCK)],
                    held.at[q // 2 * 4 + 2 * e + half],
                    sem.at[2 * q + e],
                )
            )
    for copy in copies:
        copy.start()
    from_r1 = pltpu.make_async_copy(r1.at[pl.ds(2 * BLOCK, 16)], partner, sem.at[8])
    from_rm = pltpu.make_async_copy(rm.at[pl.ds(2 * BLOCK, 16)], partner, sem.at[8])
    pl.when(a == 1)(from_r1.start)
    pl.when(a == 0)(from_rm.start)
    for copy in copies:
        copy.wait()
    from_r1.wait()

    def one(q, carry):
        low = pl.multiple_of(q // 4 * T, T)
        keys = held[q, 12 * T :, :].astype(F32)
        for i in range(3):
            tiles = [held[q, (4 * i + t) * T : (4 * i + t + 1) * T, :] for t in range(4)]
            for d in range(5):
                parts = [tiles[t] * chosen(keys[4 * i + t : 4 * i + t + 1], float(d - 2)) for t in range(4)]
                out[i, q % 4, pl.ds(low, T), d * T : (d + 1) * T] = (parts[0] + parts[1]) + (parts[2] + parts[3])
        return carry

    lax.fori_loop(0, 8, one, 0)


def left_panels(place, same, r1, rm, r2):
    return pl.pallas_call(
        left_kernel,
        out_shape=[
            jax.ShapeDtypeStruct((3, 4, 2 * T, 5 * T), BF16),
            jax.ShapeDtypeStruct((16, T), BF16),
        ],
        in_specs=[SMEM] + [ANY] * 4,
        out_specs=[VMEM, VMEM],
        scratch_shapes=[pltpu.VMEM((8, BLOCK, T), BF16), pltpu.SemaphoreType.DMA((9,))],
        compiler_params=params(),
        cost_estimate=cost(LEFT, 8 << 20),
        name="left_panels",
    )(place, same, r1, rm, r2)


EDGE_ROWS = 2 * (HEAD + TAIL)


def edge_copies(place, held, base, h, panel, outs, sem):
    core = place[3]
    copies = []
    for out, start in zip(outs, (1 - core, core)):
        for first, size, into in ((0, HEAD, 0), (3 * HEAD, TAIL, 2 * HEAD)):
            begin = pl.multiple_of(base + first + start * size, 16)
            copies.append((held.at[pl.ds(begin, 2 * size)], out.at[h, panel, pl.ds(into, 2 * size)]))
    return copies


def edge_kernel(near, place, *refs):
    outs, sem, b = refs[-3:-1], refs[-1], place[2]
    moves = []
    for h in range(2):
        if near:
            for source, panel in zip(refs[:3], (b, (b + 3) % 4, (b + 1) % 4)):
                moves += edge_copies(place, source, h * PIECE, h, panel, outs, sem)
        else:
            moves += edge_copies(place, refs[h], 0, h, (b + 2) % 4, outs, sem)
    run_all([pltpu.make_async_copy(source, into, sem.at[n]) for n, (source, into) in enumerate(moves)])


def edges(flops, place, near, sources, begun=()):
    shape = jax.ShapeDtypeStruct((2, 4, EDGE_ROWS, T), BF16)
    count = len(sources)
    return pl.pallas_call(
        functools.partial(edge_kernel, near),
        out_shape=[shape, shape],
        in_specs=[SMEM] + [ANY] * (count + len(begun)),
        out_specs=[ANY] * 2,
        input_output_aliases={count + 1 + n: n for n in range(len(begun))},
        scratch_shapes=[pltpu.SemaphoreType.DMA((24,))],
        compiler_params=params(),
        cost_estimate=cost(flops, 4 << 20),
        name="near_edges" if near else "far_edges",
    )(place, *sources, *begun)


def multiply_kernel(
    h, place, own, up, down, far0, far1, from_core, from_halo, left, mine, partner,
    keep, give, heads, tails, lefts, right, sem,
):
    b, core = place[2], place[3]
    copies = []

    def load(source, into):
        copies.append(pltpu.make_async_copy(source, into, sem.at[len(copies)]))

    for source, panel in ((own, b), (up, (b + 3) % 4), (down, (b + 1) % 4), (None, (b + 2) % 4)):
        held = (far0, far1)[h] if source is None else source
        base = 0 if source is None else h * PIECE
        load(held.at[pl.ds(base, 3 * HEAD)], heads.at[panel, pl.ds(2 * HEAD, 3 * HEAD)])
        load(held.at[pl.ds(base + 3 * HEAD, 3 * TAIL)], tails.at[panel, pl.ds(2 * TAIL, 3 * TAIL)])
    for source, slot in ((from_core, 5 * (1 - core)), (from_halo, 5 * core)):
        at = pl.ds(pl.multiple_of(slot * HEAD, 16), 2 * HEAD)
        load(source.at[h, :, pl.ds(0, 2 * HEAD)], heads.at[:, at])
        at = pl.ds(pl.multiple_of(slot * TAIL, 16), 2 * TAIL)
        load(source.at[h, :, pl.ds(2 * HEAD, 2 * TAIL)], tails.at[:, at])
    for p in range(4):
        load(left.at[:, p], lefts.at[p])
    for copy in copies:
        copy.start()
    for copy in copies[:12]:
        copy.wait()
    half = (lanes() >= T // 2).astype(F32)
    zero = jnp.zeros((T, T), BF16)
    sums = [None] * 3
    for p in range(4):
        for k in range(7):
            keys = tails[p, k * TAIL + T : (k + 1) * TAIL, :].astype(F32) + float(k)
            v0 = heads[p, k * HEAD : (k + 1) * HEAD, :]
            v1 = tails[p, k * TAIL : k * TAIL + T, :]
            w0, w1 = flipped(v0), flipped(v1)
            for w in range(4):
                into = (p % 2, slice(k * T, (k + 1) * T), slice(w * T, (w + 1) * T))
                if 2 * w + 1 < k - 2 or 2 * w > k + 2:
                    right[into] = zero
                    continue
                target = half + float(2 * w)
                pick = [chosen(keys[n : n + 1], target) for n in range(4)]
                right[into] = (v0 * pick[0] + w0 * pick[1]) + (v1 * pick[2] + w1 * pick[3])
        copies[12 + p].wait()
        for i in range(3):
            first = i // 2 * T
            part = jnp.dot(
                lefts[p, i],
                right[p % 2, i * T : (i + 5) * T, first : first + 3 * T],
                preferred_element_type=F32,
            )
            sums[i] = part if sums[i] is None else sums[i] + part
    for i in range(3):
        for side, (out, source) in enumerate(((keep, mine), (give, partner))):
            keys = source[...].astype(F32)[4 * i : 4 * i + 4] + float(i + 2)
            for m in range(2):
                total = None
                for w in range(3):
                    v = sums[i][side * T : (side + 1) * T, w * T : (w + 1) * T]
                    target = half + float(2 * (w + i // 2))
                    swap = (1.0 - half) + float(2 * (w + i // 2))
                    key = keys[2 * m : 2 * m + 1]
                    part = v * jnp.where(key == target, 1.0, 0.0)
                    part = part + turned(v) * jnp.where(key == swap, 1.0, 0.0)
                    total = part if total is None else total + part
                out[i, m] = total


def multiply(flops, h, place, sources, left, mine, partner):
    shape = jax.ShapeDtypeStruct((3, 2, T, T), F32)
    return pl.pallas_call(
        functools.partial(multiply_kernel, h),
        out_shape=[shape, shape],
        in_specs=[SMEM] + [ANY] * 8 + [VMEM] * 2,
        out_specs=[VMEM, VMEM],
        scratch_shapes=[
            pltpu.VMEM((4, 7 * HEAD, T), BF16),
            pltpu.VMEM((4, 7 * TAIL, T), BF16),
            pltpu.VMEM((4, 3, 2 * T, 5 * T), BF16),
            pltpu.VMEM((2, 7 * T, 4 * T), BF16),
            pltpu.SemaphoreType.DMA((16,)),
        ],
        compiler_params=params(),
        cost_estimate=cost(flops, 10 << 20),
        name="multiply",
    )(place, *sources, left, mine, partner)


def finish_kernel(own0, got0, own1, got1, out):
    here = lanes() < T // 2
    for i in range(3):
        for m in range(2):
            low = own0[i, m] + got0[i, m]
            high = own1[i, m] + got1[i, m]
            out[i, 2 * m] = jnp.where(here, low, turned(high)).astype(BF16)
            out[i, 2 * m + 1] = jnp.where(here, turned(low), high).astype(BF16)


def finish(own0, got0, own1, got1):
    return pl.pallas_call(
        finish_kernel,
        out_shape=jax.ShapeDtypeStruct((3, 4, T, T), BF16),
        in_specs=[VMEM] * 4,
        out_specs=VMEM,
        compiler_params=params(),
        cost_estimate=cost(1 << 20, 2 << 20),
        name="finish",
    )(own0, got0, own1, got1)


def after(value, *others):
    return lax.optimization_barrier((value,) + others)[0]


def body(x_tiles, tile_cols, tile_counts):
    row, col = lax.axis_index("row"), lax.axis_index("col")
    place = jnp.stack([row, row // 32, row // 8 % 4, row % 2, col // 2, col % 2]).astype(I32)
    block, whole, keys = pack(place, tile_cols, tile_counts, x_tiles)
    up, down = send(whole, along_z(4)), send(whole, along_z(-4))
    g1, g3, g2 = send(block, along_x(1)), send(block, along_x(-1)), send(block, along_x(2))
    same, other = sort_panels(place, block, g1, g2, g3, keys)
    far = (send(after(up[:PIECE], other), along_z(4)), send(after(down[PIECE:], other), along_z(-4)))
    begun = edges(EDGE[0], place, True, (whole, up, down))
    r1, rm, r2 = send(other, along_y(1)), send(other, along_y(-1)), send(same, along_y(2))
    left, partner = left_panels(place, same, r1, rm, r2)
    pieces = (whole, up, down, *far)
    to_core, to_halo = edges(EDGE[1], place, False, far, begun)
    pieces += (send(to_core, CORE), send(to_halo, HALO))
    kept, got = [], []
    for h in range(2):
        keep, give = multiply(MULT[h], h, place, pieces, left, keys, partner)
        kept.append(keep)
        got.append(send(give, PLANE))
    return finish(kept[0], got[0], kept[1], got[1])


def solution(mesh):
    placed = (P("row", "col", None, None), P("row", "col"), P("row", "col"))
    return jax.shard_map(
        body, mesh=mesh, in_specs=placed, out_specs=P("row", "col", None, None), check_vma=False
    )
```

```python
import functools

import jax
import jax.numpy as jnp
from jax import lax
from jax.experimental import pallas as pl
from jax.experimental.pallas import tpu as pltpu
from jax.sharding import PartitionSpec as P

BF16, F32, I32 = jnp.bfloat16, jnp.float32, jnp.int32
T = 128
EDGE = (0, 0)
MULT = (3 << 30, 3 << 30)
LEFT = 5700000000
SORT = 0
LIMIT = 48 << 20
BLOCK = 12 * T + 16
HEAD, TAIL = T, T + 16
PIECE = 3 * (HEAD + TAIL)
VMEM = pl.BlockSpec(memory_space=pltpu.VMEM)
SMEM = pl.BlockSpec(memory_space=pltpu.SMEM)


def routes(move):
    pairs = []
    for row in range(64):
        for col in range(8):
            a, z, k, x, h = move(row // 32, row // 2 % 16, row % 2, col // 2, col % 2)
            pairs.append((row * 8 + col, (a * 32 + z % 16 * 2 + k) * 8 + x % 4 * 2 + h))
    return pairs


def along_z(n):
    return routes(lambda a, z, k, x, h: (a, z + n, k, x, h))


def along_x(n):
    return routes(lambda a, z, k, x, h: (a, z, k, x + n, h))


def along_y(n):
    def move(a, z, k, x, h):
        y = (2 * h + a + n) % 4
        return y % 2, z, k, x, y // 2

    return routes(move)


CORE = routes(lambda a, z, k, x, h: (a, z, 1 - k, x, h))
HALO = routes(lambda a, z, k, x, h: (a, z + 2 * k - 1, 1 - k, x, h))
PLANE = routes(lambda a, z, k, x, h: (1 - a, z, k, x, h))


def send(block, pairs):
    return lax.ppermute(block, ("row", "col"), pairs)


def params():
    return pltpu.CompilerParams(vmem_limit_bytes=LIMIT)


def cost(flops, moved):
    return pl.CostEstimate(flops=flops, bytes_accessed=moved, transcendentals=0)


def lanes():
    return lax.broadcasted_iota(I32, (1, T), 1)


def flipped(v):
    return pltpu.roll(v, T // 2, 1)


def chosen(keys, target):
    return jnp.where(keys == target, 1.0, 0.0).astype(BF16)


def turned(v):
    return pltpu.roll(v, T // 2, 1)


def pack_kernel(place, cols, counts, x, a_out, b_out, k_out):
    row = lax.broadcasted_iota(I32, (16, T), 0)
    left = lax.broadcasted_iota(I32, (16, T), 1) < T // 2
    plain = jnp.full((16, T), 9, I32)
    paired = jnp.full((16, T), 9, I32)
    for r in range(3):
        keys = []
        for t in range(4):
            away = (cols[r, t] - (place[0] * 3 + r) + 240) % 24
            away = jnp.where(away > 12, away - 24, away)
            keys.append(jnp.where(t < counts[0, r], away, 9))
            plain = jnp.where(row == r * 4 + t, keys[t], plain)
        for m in range(2):
            first, second = keys[2 * m], keys[2 * m + 1]
            paired = jnp.where(row == r * 4 + 2 * m, jnp.where(left, first, second), paired)
            paired = jnp.where(row == r * 4 + 2 * m + 1, jnp.where(left, second, first), paired)
    a_out[12 * T :, :] = plain.astype(F32).astype(BF16)
    paired = paired.astype(F32)
    k_out[...] = paired.astype(BF16)
    here = lanes() < T // 2
    for r in range(3):
        tail = 3 * HEAD + r * TAIL
        keyed = jnp.concatenate([paired[4 * r : 4 * r + 4], jnp.full((12, T), 9.0, F32)], axis=0)
        keyed = keyed.astype(BF16)
        b_out[tail + T : tail + TAIL, :] = keyed
        b_out[PIECE + tail + T : PIECE + tail + TAIL, :] = keyed
        for m in range(2):
            at = r * HEAD if m == 0 else tail
            even = x[r, 2 * m]
            odd = x[r, 2 * m + 1]
            a_out[(4 * r + 2 * m) * T : (4 * r + 2 * m + 1) * T, :] = even
            a_out[(4 * r + 2 * m + 1) * T : (4 * r + 2 * m + 2) * T, :] = odd
            even, odd = even.astype(F32), odd.astype(F32)
            b_out[at : at + T, :] = jnp.where(here, even, turned(odd)).astype(BF16)
            b_out[PIECE + at : PIECE + at + T, :] = jnp.where(here, turned(even), odd).astype(BF16)


def pack(place, cols, counts, x):
    shapes = ((BLOCK, T), (2 * PIECE, T), (16, T))
    return pl.pallas_call(
        pack_kernel,
        out_shape=[jax.ShapeDtypeStruct(s, BF16) for s in shapes],
        in_specs=[SMEM, SMEM, SMEM, VMEM],
        out_specs=[VMEM] * 3,
        compiler_params=params(),
        cost_estimate=cost(1 << 20, 6 << 20),
        name="pack",
    )(place, cols, counts.T, x)


def sort_kernel(place, own, g1, g2, g3, keys, same, other):
    a, x = place[1], place[4]
    other[2 * BLOCK :, :] = keys[...]
    for k, source in enumerate((own, g1, g2, g3)):
        panel = (x - k + 4) % 4
        at = pl.multiple_of(panel % 2 * BLOCK, 16)

        @pl.when(panel // 2 == a)
        def _(source=source, at=at):
            same[pl.ds(at, BLOCK), :] = source[...]

        @pl.when(panel // 2 != a)
        def _(source=source, at=at):
            other[pl.ds(at, BLOCK), :] = source[...]


def sort_panels(place, own, g1, g2, g3, keys):
    return pl.pallas_call(
        sort_kernel,
        out_shape=[
            jax.ShapeDtypeStruct((2 * BLOCK, T), BF16),
            jax.ShapeDtypeStruct((2 * BLOCK + 16, T), BF16),
        ],
        in_specs=[SMEM] + [VMEM] * 5,
        out_specs=[VMEM] * 2,
        compiler_params=params(),
        cost_estimate=cost(SORT, 4 << 20),
        name="sort_panels",
    )(place, own, g1, g2, g3, keys)


def left_kernel(place, same, r1, rm, r2, out, partner):
    a, h = place[1], place[5]
    near = jnp.where(a == 1, h, 1 - h)
    keys = slice(2 * BLOCK, 2 * BLOCK + 16)
    partner[...] = jnp.where(a == 1, r1[keys, :].astype(F32), rm[keys, :].astype(F32)).astype(BF16)
    for n, (source, half) in enumerate(((same, h), (r2, 1 - h), (r1, near), (rm, 1 - near))):
        rows = slice(n // 2 * T, (n // 2 + 1) * T)

        def one(e, carry, source=source, half=half, rows=rows):
            base = pl.multiple_of(e * BLOCK, 16)
            keys = source[pl.ds(base + 12 * T, 16), :].astype(F32)
            for i in range(3):
                tiles = [source[pl.ds(base + (4 * i + t) * T, T), :] for t in range(4)]
                for d in range(5):
                    parts = [tiles[t] * chosen(keys[4 * i + t : 4 * i + t + 1], float(d - 2)) for t in range(4)]
                    block = (parts[0] + parts[1]) + (parts[2] + parts[3])
                    out[i, 2 * e + half, rows, d * T : (d + 1) * T] = block
            return carry

        lax.fori_loop(0, 2, one, 0)


def left_panels(place, same, r1, rm, r2):
    return pl.pallas_call(
        left_kernel,
        out_shape=[
            jax.ShapeDtypeStruct((3, 4, 2 * T, 5 * T), BF16),
            jax.ShapeDtypeStruct((16, T), BF16),
        ],
        in_specs=[SMEM] + [VMEM] * 4,
        out_specs=[VMEM, VMEM],
        compiler_params=params(),
        cost_estimate=cost(LEFT, 8 << 20),
        name="left_panels",
    )(place, same, r1, rm, r2)


EDGE_ROWS = 2 * (HEAD + TAIL)


def edge_kernel(place, own, up, down, far0, far1, to_core, to_halo):
    b, core = place[2], place[3]
    for out, start in ((to_core, 1 - core), (to_halo, core)):
        for source, panel in ((own, b), (up, (b + 3) % 4), (down, (b + 1) % 4), (None, (b + 2) % 4)):
            for h in range(2):
                held = (far0, far1)[h] if source is None else source
                base = 0 if source is None else h * PIECE
                for first, size, into in ((0, HEAD, 0), (3 * HEAD, TAIL, 2 * HEAD)):
                    begin = pl.multiple_of(base + first + start * size, 16)
                    out[h, panel, into : into + 2 * size, :] = held[pl.ds(begin, 2 * size), :]


def edges(flops, place, *sources):
    shape = jax.ShapeDtypeStruct((2, 4, EDGE_ROWS, T), BF16)
    return pl.pallas_call(
        edge_kernel,
        out_shape=[shape, shape],
        in_specs=[SMEM] + [VMEM] * 5,
        out_specs=[VMEM] * 2,
        compiler_params=params(),
        cost_estimate=cost(flops, 4 << 20),
        name="edges",
    )(place, *sources)


def multiply_kernel(
    h, place, own, up, down, far0, far1, from_core, from_halo, left, mine, partner, keep, give, right
):
    b, core = place[2], place[3]
    half = (lanes() >= T // 2).astype(F32)
    zero = jnp.zeros((T, T), BF16)
    sums = [None] * 3
    for p, (source, shift) in enumerate(((own, 0), (up, 3), (down, 1), (None, 2))):
        panel = (b + shift) % 4
        held = (far0, far1)[h] if source is None else source
        base = 0 if source is None else h * PIECE

        def edge(first, size, low):
            rows = slice(first, first + size)
            above, below = (from_halo, from_core) if low else (from_core, from_halo)
            return jnp.where(core == 0, above[h, panel, rows, :], below[h, panel, rows, :])

        for k in range(7):
            if 2 <= k < 5:
                head = base + (k - 2) * HEAD
                tail = base + 3 * HEAD + (k - 2) * TAIL
                v0 = held[head : head + T, :]
                v1 = held[tail : tail + T, :]
                keys = held[tail + T : tail + TAIL, :]
            else:
                row, low = (k, True) if k < 2 else (k - 5, False)
                v0 = edge(row * HEAD, T, low)
                v1 = edge(2 * HEAD + row * TAIL, T, low)
                keys = edge(2 * HEAD + row * TAIL + T, 16, low)
            keys = keys.astype(F32) + float(k)
            w0, w1 = flipped(v0), flipped(v1)
            for w in range(4):
                into = (p % 2, slice(k * T, (k + 1) * T), slice(w * T, (w + 1) * T))
                if 2 * w + 1 < k - 2 or 2 * w > k + 2:
                    if p < 2:
                        right[into] = zero
                    continue
                target = half + float(2 * w)
                pick = [chosen(keys[n : n + 1], target) for n in range(4)]
                right[into] = (v0 * pick[0] + w0 * pick[1]) + (v1 * pick[2] + w1 * pick[3])
        for i in range(3):
            first = i // 2 * T
            part = jnp.dot(
                left[i, panel],
                right[p % 2, i * T : (i + 5) * T, first : first + 3 * T],
                preferred_element_type=F32,
            )
            sums[i] = part if sums[i] is None else sums[i] + part
    for i in range(3):
        for side, (out, source) in enumerate(((keep, mine), (give, partner))):
            keys = source[...].astype(F32)[4 * i : 4 * i + 4] + float(i + 2)
            for m in range(2):
                total = None
                for w in range(3):
                    v = sums[i][side * T : (side + 1) * T, w * T : (w + 1) * T]
                    target = half + float(2 * (w + i // 2))
                    swap = (1.0 - half) + float(2 * (w + i // 2))
                    key = keys[2 * m : 2 * m + 1]
                    part = v * jnp.where(key == target, 1.0, 0.0)
                    part = part + turned(v) * jnp.where(key == swap, 1.0, 0.0)
                    total = part if total is None else total + part
                out[i, m] = total


def multiply(flops, h, place, sources, left, mine, partner):
    shape = jax.ShapeDtypeStruct((3, 2, T, T), F32)
    return pl.pallas_call(
        functools.partial(multiply_kernel, h),
        out_shape=[shape, shape],
        in_specs=[SMEM] + [VMEM] * 10,
        out_specs=[VMEM, VMEM],
        scratch_shapes=[pltpu.VMEM((2, 7 * T, 4 * T), BF16)],
        compiler_params=params(),
        cost_estimate=cost(flops, 10 << 20),
        name="multiply",
    )(place, *sources, left, mine, partner)


def finish_kernel(own0, got0, own1, got1, out):
    here = lanes() < T // 2
    for i in range(3):
        for m in range(2):
            low = own0[i, m] + got0[i, m]
            high = own1[i, m] + got1[i, m]
            out[i, 2 * m] = jnp.where(here, low, turned(high)).astype(BF16)
            out[i, 2 * m + 1] = jnp.where(here, turned(low), high).astype(BF16)


def finish(own0, got0, own1, got1):
    return pl.pallas_call(
        finish_kernel,
        out_shape=jax.ShapeDtypeStruct((3, 4, T, T), BF16),
        in_specs=[VMEM] * 4,
        out_specs=VMEM,
        compiler_params=params(),
        cost_estimate=cost(1 << 20, 2 << 20),
        name="finish",
    )(own0, got0, own1, got1)


def after(value, *others):
    return lax.optimization_barrier((value,) + others)[0]


def body(x_tiles, tile_cols, tile_counts):
    row, col = lax.axis_index("row"), lax.axis_index("col")
    place = jnp.stack([row, row // 32, row // 8 % 4, row % 2, col // 2, col % 2]).astype(I32)
    block, whole, keys = pack(place, tile_cols, tile_counts, x_tiles)
    up, down = send(whole, along_z(4)), send(whole, along_z(-4))
    g1, g3, g2 = send(block, along_x(1)), send(block, along_x(-1)), send(block, along_x(2))
    same, other = sort_panels(place, block, g1, g2, g3, keys)
    far = (send(after(up[:PIECE], other), along_z(4)), send(after(down[PIECE:], other), along_z(-4)))
    r1, rm, r2 = send(other, along_y(1)), send(other, along_y(-1)), send(same, along_y(2))
    left, partner = left_panels(place, same, r1, rm, r2)
    pieces = (whole, up, down, *far)
    to_core, to_halo = edges(EDGE[0], place, *pieces)
    pieces += (send(to_core, CORE), send(to_halo, HALO))
    kept, got = [], []
    for h in range(2):
        keep, give = multiply(MULT[h], h, place, pieces, left, keys, partner)
        kept.append(keep)
        got.append(send(give, PLANE))
    return finish(kept[0], got[0], kept[1], got[1])


def solution(mesh):
    placed = (P("row", "col", None, None), P("row", "col"), P("row", "col"))
    return jax.shard_map(
        body, mesh=mesh, in_specs=placed, out_specs=P("row", "col", None, None), check_vma=False
    )
```

```python
import functools

import jax
import jax.numpy as jnp
from jax import lax
from jax.experimental import pallas as pl
from jax.experimental.pallas import tpu as pltpu
from jax.sharding import PartitionSpec as P

BF16, F32, I32 = jnp.bfloat16, jnp.float32, jnp.int32
T = 128
EDGE = (0, 0)
MULT = (3 << 30, 3 << 30)
LEFT = 5700000000
SORT = 0
BEGIN = 0
LIMIT = 48 << 20
BLOCK = 12 * T + 16
HEAD, TAIL = T, T + 16
PIECE = 3 * (HEAD + TAIL)
VMEM = pl.BlockSpec(memory_space=pltpu.VMEM)
SMEM = pl.BlockSpec(memory_space=pltpu.SMEM)


def routes(move):
    pairs = []
    for row in range(64):
        for col in range(8):
            a, z, k, x, h = move(row // 32, row // 2 % 16, row % 2, col // 2, col % 2)
            pairs.append((row * 8 + col, (a * 32 + z % 16 * 2 + k) * 8 + x % 4 * 2 + h))
    return pairs


def along_z(n):
    return routes(lambda a, z, k, x, h: (a, z + n, k, x, h))


def along_x(n):
    return routes(lambda a, z, k, x, h: (a, z, k, x + n, h))


def along_y(n):
    def move(a, z, k, x, h):
        y = (2 * h + a + n) % 4
        return y % 2, z, k, x, y // 2

    return routes(move)


CORE = routes(lambda a, z, k, x, h: (a, z, 1 - k, x, h))
HALO = routes(lambda a, z, k, x, h: (a, z + 2 * k - 1, 1 - k, x, h))
PLANE = routes(lambda a, z, k, x, h: (1 - a, z, k, x, h))


def send(block, pairs):
    return lax.ppermute(block, ("row", "col"), pairs)


def params():
    return pltpu.CompilerParams(vmem_limit_bytes=LIMIT)


def cost(flops, moved):
    return pl.CostEstimate(flops=flops, bytes_accessed=moved, transcendentals=0)


def lanes():
    return lax.broadcasted_iota(I32, (1, T), 1)


def flipped(v):
    return pltpu.roll(v, T // 2, 1)


def chosen(keys, target):
    return jnp.where(keys == target, 1.0, 0.0).astype(BF16)


def turned(v):
    return pltpu.roll(v, T // 2, 1)


def pack_kernel(place, cols, counts, x, a_out, b_out, k_out):
    row = lax.broadcasted_iota(I32, (16, T), 0)
    left = lax.broadcasted_iota(I32, (16, T), 1) < T // 2
    plain = jnp.full((16, T), 9, I32)
    paired = jnp.full((16, T), 9, I32)
    for r in range(3):
        keys = []
        for t in range(4):
            away = (cols[r, t] - (place[0] * 3 + r) + 240) % 24
            away = jnp.where(away > 12, away - 24, away)
            keys.append(jnp.where(t < counts[0, r], away, 9))
            plain = jnp.where(row == r * 4 + t, keys[t], plain)
        for m in range(2):
            first, second = keys[2 * m], keys[2 * m + 1]
            paired = jnp.where(row == r * 4 + 2 * m, jnp.where(left, first, second), paired)
            paired = jnp.where(row == r * 4 + 2 * m + 1, jnp.where(left, second, first), paired)
    a_out[12 * T :, :] = plain.astype(F32).astype(BF16)
    paired = paired.astype(F32)
    k_out[...] = paired.astype(BF16)
    here = lanes() < T // 2
    for r in range(3):
        tail = 3 * HEAD + r * TAIL
        keyed = jnp.concatenate([paired[4 * r : 4 * r + 4], jnp.full((12, T), 9.0, F32)], axis=0)
        keyed = keyed.astype(BF16)
        b_out[tail + T : tail + TAIL, :] = keyed
        b_out[PIECE + tail + T : PIECE + tail + TAIL, :] = keyed
        for m in range(2):
            at = r * HEAD if m == 0 else tail
            even = x[r, 2 * m]
            odd = x[r, 2 * m + 1]
            a_out[(4 * r + 2 * m) * T : (4 * r + 2 * m + 1) * T, :] = even
            a_out[(4 * r + 2 * m + 1) * T : (4 * r + 2 * m + 2) * T, :] = odd
            even, odd = even.astype(F32), odd.astype(F32)
            b_out[at : at + T, :] = jnp.where(here, even, turned(odd)).astype(BF16)
            b_out[PIECE + at : PIECE + at + T, :] = jnp.where(here, turned(even), odd).astype(BF16)


def pack(place, cols, counts, x):
    shapes = ((BLOCK, T), (2 * PIECE, T), (16, T))
    return pl.pallas_call(
        pack_kernel,
        out_shape=[jax.ShapeDtypeStruct(s, BF16) for s in shapes],
        in_specs=[SMEM, SMEM, SMEM, VMEM],
        out_specs=[VMEM] * 3,
        compiler_params=params(),
        cost_estimate=cost(1 << 20, 6 << 20),
        name="pack",
    )(place, cols, counts.T, x)


def sort_kernel(place, own, g1, g2, g3, keys, same, other):
    a, x = place[1], place[4]
    other[2 * BLOCK :, :] = keys[...]
    for k, source in enumerate((own, g1, g2, g3)):
        panel = (x - k + 4) % 4
        at = pl.multiple_of(panel % 2 * BLOCK, 16)

        @pl.when(panel // 2 == a)
        def _(source=source, at=at):
            same[pl.ds(at, BLOCK), :] = source[...]

        @pl.when(panel // 2 != a)
        def _(source=source, at=at):
            other[pl.ds(at, BLOCK), :] = source[...]


def sort_panels(place, own, g1, g2, g3, keys):
    return pl.pallas_call(
        sort_kernel,
        out_shape=[
            jax.ShapeDtypeStruct((2 * BLOCK, T), BF16),
            jax.ShapeDtypeStruct((2 * BLOCK + 16, T), BF16),
        ],
        in_specs=[SMEM] + [VMEM] * 5,
        out_specs=[VMEM] * 2,
        compiler_params=params(),
        cost_estimate=cost(SORT, 4 << 20),
        name="sort_panels",
    )(place, own, g1, g2, g3, keys)


def left_kernel(place, same, r1, rm, r2, out, partner):
    a, h = place[1], place[5]
    near = jnp.where(a == 1, h, 1 - h)
    keys = slice(2 * BLOCK, 2 * BLOCK + 16)
    partner[...] = jnp.where(a == 1, r1[keys, :].astype(F32), rm[keys, :].astype(F32)).astype(BF16)
    for n, (source, half) in enumerate(((same, h), (r2, 1 - h), (r1, near), (rm, 1 - near))):
        rows = slice(n // 2 * T, (n // 2 + 1) * T)

        def one(e, carry, source=source, half=half, rows=rows):
            base = pl.multiple_of(e * BLOCK, 16)
            keys = source[pl.ds(base + 12 * T, 16), :].astype(F32)
            for i in range(3):
                tiles = [source[pl.ds(base + (4 * i + t) * T, T), :] for t in range(4)]
                for d in range(5):
                    parts = [tiles[t] * chosen(keys[4 * i + t : 4 * i + t + 1], float(d - 2)) for t in range(4)]
                    block = (parts[0] + parts[1]) + (parts[2] + parts[3])
                    out[i, 2 * e + half, rows, d * T : (d + 1) * T] = block
            return carry

        lax.fori_loop(0, 2, one, 0)


def left_panels(place, same, r1, rm, r2):
    return pl.pallas_call(
        left_kernel,
        out_shape=[
            jax.ShapeDtypeStruct((3, 4, 2 * T, 5 * T), BF16),
            jax.ShapeDtypeStruct((16, T), BF16),
        ],
        in_specs=[SMEM] + [VMEM] * 4,
        out_specs=[VMEM, VMEM],
        compiler_params=params(),
        cost_estimate=cost(LEFT, 8 << 20),
        name="left_panels",
    )(place, same, r1, rm, r2)


EDGE_ROWS = 2 * (HEAD + TAIL)


def edge_kernel(place, own, up, down, far0, far1, to_core, to_halo):
    b, core = place[2], place[3]
    for out, start in ((to_core, 1 - core), (to_halo, core)):
        for source, panel in ((own, b), (up, (b + 3) % 4), (down, (b + 1) % 4), (None, (b + 2) % 4)):
            for h in range(2):
                held = (far0, far1)[h] if source is None else source
                base = 0 if source is None else h * PIECE
                for first, size, into in ((0, HEAD, 0), (3 * HEAD, TAIL, 2 * HEAD)):
                    begin = pl.multiple_of(base + first + start * size, 16)
                    out[h, panel, into : into + 2 * size, :] = held[pl.ds(begin, 2 * size), :]


def edges(flops, place, *sources):
    shape = jax.ShapeDtypeStruct((2, 4, EDGE_ROWS, T), BF16)
    return pl.pallas_call(
        edge_kernel,
        out_shape=[shape, shape],
        in_specs=[SMEM] + [VMEM] * 5,
        out_specs=[VMEM] * 2,
        compiler_params=params(),
        cost_estimate=cost(flops, 4 << 20),
        name="edges",
    )(place, *sources)


def place_row(k, v0, v1, keys, right, at, row, clear):
    half = (lanes() >= T // 2).astype(F32)
    keys = keys.astype(F32) + float(k)
    w0, w1 = flipped(v0), flipped(v1)
    for w in range(4):
        into = (at, slice(row * T, (row + 1) * T), slice(w * T, (w + 1) * T))
        if 2 * w + 1 < k - 2 or 2 * w > k + 2:
            if clear:
                right[into] = jnp.zeros((T, T), BF16)
            continue
        pick = [chosen(keys[n : n + 1], half + float(2 * w)) for n in range(4)]
        right[into] = (v0 * pick[0] + w0 * pick[1]) + (v1 * pick[2] + w1 * pick[3])


def begin_kernel(h, place, own, up, down, far0, far1, left, out, right):
    sums = [None] * 3
    for p, (source, shift) in enumerate(((own, 0), (up, 3), (down, 1), (None, 2))):
        panel = (place[2] + shift) % 4
        held = (far0, far1)[h] if source is None else source
        base = 0 if source is None else h * PIECE
        for r in range(3):
            head = base + r * HEAD
            tail = base + 3 * HEAD + r * TAIL
            keys = held[tail + T : tail + TAIL, :]
            place_row(r + 2, held[head : head + T, :], held[tail : tail + T, :], keys, right, p % 2, r, p < 2)
        for i in range(3):
            first = i // 2 * T
            part = jnp.dot(
                left[i, panel, :, (2 - i) * T : (5 - i) * T],
                right[p % 2, :, first : first + 3 * T],
                preferred_element_type=F32,
            )
            sums[i] = part if sums[i] is None else sums[i] + part
    for i in range(3):
        out[i] = sums[i]


def begin(flops, h, place, pieces, left):
    return pl.pallas_call(
        functools.partial(begin_kernel, h),
        out_shape=jax.ShapeDtypeStruct((3, 2 * T, 3 * T), F32),
        in_specs=[SMEM] + [VMEM] * 6,
        out_specs=VMEM,
        scratch_shapes=[pltpu.VMEM((2, 3 * T, 4 * T), BF16)],
        compiler_params=params(),
        cost_estimate=cost(flops, 6 << 20),
        name="begin",
    )(place, *pieces, left)


def multiply_kernel(h, place, from_core, from_halo, begun, left, mine, partner, keep, give, right):
    b, core = place[2], place[3]
    half = (lanes() >= T // 2).astype(F32)
    sums = [begun[i] for i in range(3)]
    for panel in range(4):

        def edge(first, size, low, panel=panel):
            rows = slice(first, first + size)
            above, below = (from_halo, from_core) if low else (from_core, from_halo)
            return jnp.where(core == 0, above[h, panel, rows, :], below[h, panel, rows, :])

        for n, k in enumerate((0, 1, 5, 6)):
            row, low = n % 2, n < 2
            tail = 2 * HEAD + row * TAIL
            keys = edge(tail + T, 16, low)
            place_row(k, edge(row * HEAD, T, low), edge(tail, T, low), keys, right, panel % 2, n, panel < 2)
        for i in range(3):
            first = i // 2 * T
            side = left[i, panel]
            if i == 1:
                side = jnp.concatenate([side[:, :T], side[:, 4 * T :]], axis=1)
            else:
                side = side[:, : 2 * T] if i == 0 else side[:, 3 * T :]
            sums[i] = sums[i] + jnp.dot(
                side,
                right[panel % 2, i * T : (i + 2) * T, first : first + 3 * T],
                preferred_element_type=F32,
            )
    for i in range(3):
        for side, (out, source) in enumerate(((keep, mine), (give, partner))):
            keys = source[...].astype(F32)[4 * i : 4 * i + 4] + float(i + 2)
            for m in range(2):
                total = None
                for w in range(3):
                    v = sums[i][side * T : (side + 1) * T, w * T : (w + 1) * T]
                    target = half + float(2 * (w + i // 2))
                    swap = (1.0 - half) + float(2 * (w + i // 2))
                    key = keys[2 * m : 2 * m + 1]
                    part = v * jnp.where(key == target, 1.0, 0.0)
                    part = part + turned(v) * jnp.where(key == swap, 1.0, 0.0)
                    total = part if total is None else total + part
                out[i, m] = total


def multiply(flops, h, place, received, begun, left, mine, partner):
    shape = jax.ShapeDtypeStruct((3, 2, T, T), F32)
    return pl.pallas_call(
        functools.partial(multiply_kernel, h),
        out_shape=[shape, shape],
        in_specs=[SMEM] + [VMEM] * 6,
        out_specs=[VMEM, VMEM],
        scratch_shapes=[pltpu.VMEM((2, 4 * T, 4 * T), BF16)],
        compiler_params=params(),
        cost_estimate=cost(flops, 10 << 20),
        name="multiply",
    )(place, *received, begun, left, mine, partner)


def finish_kernel(own0, got0, own1, got1, out):
    here = lanes() < T // 2
    for i in range(3):
        for m in range(2):
            low = own0[i, m] + got0[i, m]
            high = own1[i, m] + got1[i, m]
            out[i, 2 * m] = jnp.where(here, low, turned(high)).astype(BF16)
            out[i, 2 * m + 1] = jnp.where(here, turned(low), high).astype(BF16)


def finish(own0, got0, own1, got1):
    return pl.pallas_call(
        finish_kernel,
        out_shape=jax.ShapeDtypeStruct((3, 4, T, T), BF16),
        in_specs=[VMEM] * 4,
        out_specs=VMEM,
        compiler_params=params(),
        cost_estimate=cost(1 << 20, 2 << 20),
        name="finish",
    )(own0, got0, own1, got1)


def after(value, *others):
    return lax.optimization_barrier((value,) + others)[0]


def body(x_tiles, tile_cols, tile_counts):
    row, col = lax.axis_index("row"), lax.axis_index("col")
    place = jnp.stack([row, row // 32, row // 8 % 4, row % 2, col // 2, col % 2]).astype(I32)
    block, whole, keys = pack(place, tile_cols, tile_counts, x_tiles)
    up, down = send(whole, along_z(4)), send(whole, along_z(-4))
    g1, g3, g2 = send(block, along_x(1)), send(block, along_x(-1)), send(block, along_x(2))
    same, other = sort_panels(place, block, g1, g2, g3, keys)
    far = (send(after(up[:PIECE], other), along_z(4)), send(after(down[PIECE:], other), along_z(-4)))
    r1, rm, r2 = send(other, along_y(1)), send(other, along_y(-1)), send(same, along_y(2))
    left, partner = left_panels(place, same, r1, rm, r2)
    pieces = (whole, up, down, *far)
    to_core, to_halo = edges(EDGE[0], place, *pieces)
    received = (send(to_core, CORE), send(to_halo, HALO))
    begun = [begin(BEGIN, h, place, pieces, left) for h in range(2)]
    kept, got = [], []
    for h in range(2):
        keep, give = multiply(MULT[h], h, place, received, begun[h], left, keys, partner)
        kept.append(keep)
        got.append(send(give, PLANE))
    return finish(kept[0], got[0], kept[1], got[1])


def solution(mesh):
    placed = (P("row", "col", None, None), P("row", "col"), P("row", "col"))
    return jax.shard_map(
        body, mesh=mesh, in_specs=placed, out_specs=P("row", "col", None, None), check_vma=False
    )
```

```python
import functools

import jax
import jax.numpy as jnp
from jax import lax
from jax.experimental import pallas as pl
from jax.experimental.pallas import tpu as pltpu
from jax.sharding import PartitionSpec as P

BF16, F32, I32 = jnp.bfloat16, jnp.float32, jnp.int32
T = 128
MULT = (3 << 30, 3 << 30)
LEFT = 4 * 10**9
SORT = 0
EDGE = 0
BEGIN = 0
LIMIT = 48 << 20
BLOCK = 12 * T + 16
HEAD, TAIL = T, T + 16
PIECE = 3 * (HEAD + TAIL)
VMEM = pl.BlockSpec(memory_space=pltpu.VMEM)
SMEM = pl.BlockSpec(memory_space=pltpu.SMEM)


def routes(move):
    pairs = []
    for row in range(64):
        for col in range(8):
            a, z, k, x, h = move(row // 32, row // 2 % 16, row % 2, col // 2, col % 2)
            pairs.append((row * 8 + col, (a * 32 + z % 16 * 2 + k) * 8 + x % 4 * 2 + h))
    return pairs


def along_z(n):
    return routes(lambda a, z, k, x, h: (a, z + n, k, x, h))


def along_x(n):
    return routes(lambda a, z, k, x, h: (a, z, k, x + n, h))


def along_y(n):
    def move(a, z, k, x, h):
        y = (2 * h + a + n) % 4
        return y % 2, z, k, x, y // 2

    return routes(move)


CORE = routes(lambda a, z, k, x, h: (a, z, 1 - k, x, h))
HALO = routes(lambda a, z, k, x, h: (a, z + 2 * k - 1, 1 - k, x, h))
PLANE = routes(lambda a, z, k, x, h: (1 - a, z, k, x, h))


def send(block, pairs):
    return lax.ppermute(block, ("row", "col"), pairs)


def params():
    return pltpu.CompilerParams(vmem_limit_bytes=LIMIT)


def cost(flops, moved):
    return pl.CostEstimate(flops=flops, bytes_accessed=moved, transcendentals=0)


def lanes():
    return lax.broadcasted_iota(I32, (1, T), 1)


def flipped(v):
    return pltpu.roll(v, T // 2, 1)


def chosen(keys, target):
    return jnp.where(keys == target, 1.0, 0.0).astype(BF16)


def turned(v):
    return pltpu.roll(v, T // 2, 1)


def pack_kernel(place, cols, counts, x, a_out, b_out, k_out):
    row = lax.broadcasted_iota(I32, (16, T), 0)
    left = lax.broadcasted_iota(I32, (16, T), 1) < T // 2
    plain = jnp.full((16, T), 9, I32)
    paired = jnp.full((16, T), 9, I32)
    for r in range(3):
        keys = []
        for t in range(4):
            away = (cols[r, t] - (place[0] * 3 + r) + 240) % 24
            away = jnp.where(away > 12, away - 24, away)
            keys.append(jnp.where(t < counts[0, r], away, 9))
            plain = jnp.where(row == r * 4 + t, keys[t], plain)
        for m in range(2):
            first, second = keys[2 * m], keys[2 * m + 1]
            paired = jnp.where(row == r * 4 + 2 * m, jnp.where(left, first, second), paired)
            paired = jnp.where(row == r * 4 + 2 * m + 1, jnp.where(left, second, first), paired)
    a_out[12 * T :, :] = plain.astype(F32).astype(BF16)
    paired = paired.astype(F32)
    k_out[...] = paired.astype(BF16)
    here = lanes() < T // 2
    for r in range(3):
        tail = 3 * HEAD + r * TAIL
        keyed = jnp.concatenate([paired[4 * r : 4 * r + 4], jnp.full((12, T), 9.0, F32)], axis=0)
        keyed = keyed.astype(BF16)
        b_out[tail + T : tail + TAIL, :] = keyed
        b_out[PIECE + tail + T : PIECE + tail + TAIL, :] = keyed
        for m in range(2):
            at = r * HEAD if m == 0 else tail
            even = x[r, 2 * m]
            odd = x[r, 2 * m + 1]
            a_out[(4 * r + 2 * m) * T : (4 * r + 2 * m + 1) * T, :] = even
            a_out[(4 * r + 2 * m + 1) * T : (4 * r + 2 * m + 2) * T, :] = odd
            even, odd = even.astype(F32), odd.astype(F32)
            b_out[at : at + T, :] = jnp.where(here, even, turned(odd)).astype(BF16)
            b_out[PIECE + at : PIECE + at + T, :] = jnp.where(here, turned(even), odd).astype(BF16)


def pack(place, cols, counts, x):
    shapes = ((BLOCK, T), (2 * PIECE, T), (16, T))
    return pl.pallas_call(
        pack_kernel,
        out_shape=[jax.ShapeDtypeStruct(s, BF16) for s in shapes],
        in_specs=[SMEM, SMEM, SMEM, VMEM],
        out_specs=[VMEM] * 3,
        compiler_params=params(),
        cost_estimate=cost(1 << 20, 6 << 20),
        name="pack",
    )(place, cols, counts.T, x)


def sort_kernel(place, own, g1, g2, g3, keys, same, other):
    a, x = place[1], place[4]
    other[2 * BLOCK :, :] = keys[...]
    for k, source in enumerate((own, g1, g2, g3)):
        panel = (x - k + 4) % 4
        at = pl.multiple_of(panel % 2 * BLOCK, 16)

        @pl.when(panel // 2 == a)
        def _(source=source, at=at):
            same[pl.ds(at, BLOCK), :] = source[...]

        @pl.when(panel // 2 != a)
        def _(source=source, at=at):
            other[pl.ds(at, BLOCK), :] = source[...]


def sort_panels(place, own, g1, g2, g3, keys):
    return pl.pallas_call(
        sort_kernel,
        out_shape=[
            jax.ShapeDtypeStruct((2 * BLOCK, T), BF16),
            jax.ShapeDtypeStruct((2 * BLOCK + 16, T), BF16),
        ],
        in_specs=[SMEM] + [VMEM] * 5,
        out_specs=[VMEM] * 2,
        compiler_params=params(),
        cost_estimate=cost(SORT, 4 << 20),
        name="sort_panels",
    )(place, own, g1, g2, g3, keys)


def left_kernel(place, same, r1, rm, r2, out, partner):
    a, h = place[1], place[5]
    near = jnp.where(a == 1, h, 1 - h)
    keys = slice(2 * BLOCK, 2 * BLOCK + 16)
    partner[...] = jnp.where(a == 1, r1[keys, :].astype(F32), rm[keys, :].astype(F32)).astype(BF16)
    for n, (source, half) in enumerate(((same, h), (r2, 1 - h), (r1, near), (rm, 1 - near))):
        rows = slice(n // 2 * T, (n // 2 + 1) * T)

        def one(e, carry, source=source, half=half, rows=rows):
            base = pl.multiple_of(e * BLOCK, 16)
            keys = source[pl.ds(base + 12 * T, 16), :].astype(F32)
            for i in range(3):
                tiles = [source[pl.ds(base + (4 * i + t) * T, T), :] for t in range(4)]
                for d in range(5):
                    parts = [tiles[t] * chosen(keys[4 * i + t : 4 * i + t + 1], float(d - 2)) for t in range(4)]
                    block = (parts[0] + parts[1]) + (parts[2] + parts[3])
                    out[i, 2 * e + half, rows, d * T : (d + 1) * T] = block
            return carry

        lax.fori_loop(0, 2, one, 0)


def left_panels(place, same, r1, rm, r2):
    return pl.pallas_call(
        left_kernel,
        out_shape=[
            jax.ShapeDtypeStruct((3, 4, 2 * T, 5 * T), BF16),
            jax.ShapeDtypeStruct((16, T), BF16),
        ],
        in_specs=[SMEM] + [VMEM] * 4,
        out_specs=[VMEM, VMEM],
        compiler_params=params(),
        cost_estimate=cost(LEFT, 8 << 20),
        name="left_panels",
    )(place, same, r1, rm, r2)


EDGE_ROWS = 2 * (HEAD + TAIL)


def edge_kernel(near, place, *refs):
    core = place[3]
    for out, start in ((refs[-2], 1 - core), (refs[-1], core)):
        for h in range(2):
            for n, held in enumerate(refs[:3] if near else refs[h : h + 1]):
                base = h * PIECE if near else 0
                for first, size, into in ((0, HEAD, 0), (3 * HEAD, TAIL, 2 * HEAD)):
                    begin = pl.multiple_of(base + first + start * size, 16)
                    out[h, n, into : into + 2 * size, :] = held[pl.ds(begin, 2 * size), :]


def edges(near, place, *sources):
    shape = jax.ShapeDtypeStruct((2, 3 if near else 1, EDGE_ROWS, T), BF16)
    return pl.pallas_call(
        functools.partial(edge_kernel, near),
        out_shape=[shape, shape],
        in_specs=[SMEM] + [VMEM] * len(sources),
        out_specs=[VMEM] * 2,
        compiler_params=params(),
        cost_estimate=cost(EDGE if near else 0, 4 << 20),
        name="near_edges" if near else "far_edges",
    )(place, *sources)


def edge_panels(place, shift):
    core, b = place[3], place[2]
    beside = ((place[6] + 2 * core + 15) % 16 // 4 + shift) % 4
    inside = (b + shift) % 4
    return jnp.where(core == 0, beside, inside), jnp.where(core == 0, inside, beside)


def place_edges(place, h, n, from_core, from_halo, right, at, slots, clear):
    core = place[3]
    for k, slot in zip((0, 1, 5, 6), slots):
        row, low = (k, True) if k < 2 else (k - 5, False)
        above, below = (from_halo, from_core) if low else (from_core, from_halo)

        def edge(first, size, above=above, below=below):
            rows = slice(first, first + size)
            return jnp.where(core == 0, above[h, n, rows, :], below[h, n, rows, :])

        tail = 2 * HEAD + row * TAIL
        place_row(k, edge(row * HEAD, T), edge(tail, T), edge(tail + T, 16), right, at, slot, clear)


def place_row(k, v0, v1, keys, right, at, row, clear):
    half = (lanes() >= T // 2).astype(F32)
    keys = keys.astype(F32) + float(k)
    w0, w1 = flipped(v0), flipped(v1)
    for w in range(4):
        into = (at, slice(row * T, (row + 1) * T), slice(w * T, (w + 1) * T))
        if 2 * w + 1 < k - 2 or 2 * w > k + 2:
            if clear:
                right[into] = jnp.zeros((T, T), BF16)
            continue
        pick = [chosen(keys[n : n + 1], half + float(2 * w)) for n in range(4)]
        right[into] = (v0 * pick[0] + w0 * pick[1]) + (v1 * pick[2] + w1 * pick[3])


def begin_kernel(h, place, own, up, down, far0, far1, near_core, near_halo, left, out, right):
    sums = [None] * 3
    for n, (source, shift) in enumerate(((own, 0), (up, 3), (down, 1), (None, 2))):
        panel = (place[2] + shift) % 4
        held = (far0, far1)[h] if source is None else source
        base = 0 if source is None else h * PIECE
        low, high = edge_panels(place, shift)
        for r in range(3):
            head = base + r * HEAD
            tail = base + 3 * HEAD + r * TAIL
            keys = held[tail + T : tail + TAIL, :]
            place_row(r + 2, held[head : head + T, :], held[tail : tail + T, :], keys, right, n % 2, r + 2, n < 2)
        if n < 3:
            place_edges(place, h, n, near_core, near_halo, right, n % 2, (0, 1, 5, 6), n < 2)
        for i in range(3):
            first = i // 2 * T
            side = left[i, panel, :, (2 - i) * T : (5 - i) * T]
            rows = slice(2 * T, 5 * T)
            if n < 3:
                parts = [side]
                if i < 2:
                    parts = [left[i, low, :, : (2 - i) * T]] + parts
                if i > 0:
                    parts = parts + [left[i, high, :, (5 - i) * T :]]
                side = jnp.concatenate(parts, axis=1)
                rows = slice(i * T, (i + 5) * T)
            part = jnp.dot(side, right[n % 2, rows, first : first + 3 * T], preferred_element_type=F32)
            sums[i] = part if sums[i] is None else sums[i] + part
    for i in range(3):
        out[i] = sums[i]


def begin(flops, h, place, pieces, near, left):
    return pl.pallas_call(
        functools.partial(begin_kernel, h),
        out_shape=jax.ShapeDtypeStruct((3, 2 * T, 3 * T), F32),
        in_specs=[SMEM] + [VMEM] * 8,
        out_specs=VMEM,
        scratch_shapes=[pltpu.VMEM((2, 7 * T, 4 * T), BF16)],
        compiler_params=params(),
        cost_estimate=cost(flops, 6 << 20),
        name="begin",
    )(place, *pieces, *near, left)


def multiply_kernel(h, place, from_core, from_halo, begun, left, mine, partner, keep, give, right):
    half = (lanes() >= T // 2).astype(F32)
    low, high = edge_panels(place, 2)
    place_edges(place, h, 0, from_core, from_halo, right, 0, (0, 1, 2, 3), True)
    sums = []
    for i in range(3):
        first = i // 2 * T
        parts = [left[i, low, :, : (2 - i) * T]] if i < 2 else []
        parts += [left[i, high, :, (5 - i) * T :]] if i > 0 else []
        side = jnp.concatenate(parts, axis=1) if len(parts) > 1 else parts[0]
        part = jnp.dot(side, right[0, i * T : (i + 2) * T, first : first + 3 * T], preferred_element_type=F32)
        sums.append(begun[i] + part)
    for i in range(3):
        for side, (out, source) in enumerate(((keep, mine), (give, partner))):
            keys = source[...].astype(F32)[4 * i : 4 * i + 4] + float(i + 2)
            for m in range(2):
                total = None
                for w in range(3):
                    v = sums[i][side * T : (side + 1) * T, w * T : (w + 1) * T]
                    target = half + float(2 * (w + i // 2))
                    swap = (1.0 - half) + float(2 * (w + i // 2))
                    key = keys[2 * m : 2 * m + 1]
                    part = v * jnp.where(key == target, 1.0, 0.0)
                    part = part + turned(v) * jnp.where(key == swap, 1.0, 0.0)
                    total = part if total is None else total + part
                out[i, m] = total


def multiply(flops, h, place, received, begun, left, mine, partner):
    shape = jax.ShapeDtypeStruct((3, 2, T, T), F32)
    return pl.pallas_call(
        functools.partial(multiply_kernel, h),
        out_shape=[shape, shape],
        in_specs=[SMEM] + [VMEM] * 6,
        out_specs=[VMEM, VMEM],
        scratch_shapes=[pltpu.VMEM((1, 4 * T, 4 * T), BF16)],
        compiler_params=params(),
        cost_estimate=cost(flops, 10 << 20),
        name="multiply",
    )(place, *received, begun, left, mine, partner)


def finish_kernel(own0, got0, own1, got1, out):
    here = lanes() < T // 2
    for i in range(3):
        for m in range(2):
            low = own0[i, m] + got0[i, m]
            high = own1[i, m] + got1[i, m]
            out[i, 2 * m] = jnp.where(here, low, turned(high)).astype(BF16)
            out[i, 2 * m + 1] = jnp.where(here, turned(low), high).astype(BF16)


def finish(own0, got0, own1, got1):
    return pl.pallas_call(
        finish_kernel,
        out_shape=jax.ShapeDtypeStruct((3, 4, T, T), BF16),
        in_specs=[VMEM] * 4,
        out_specs=VMEM,
        compiler_params=params(),
        cost_estimate=cost(1 << 20, 2 << 20),
        name="finish",
    )(own0, got0, own1, got1)


def after(value, *others):
    return lax.optimization_barrier((value,) + others)[0]


def body(x_tiles, tile_cols, tile_counts):
    row, col = lax.axis_index("row"), lax.axis_index("col")
    place = jnp.stack([row, row // 32, row // 8 % 4, row % 2, col // 2, col % 2, row // 2 % 16]).astype(I32)
    block, whole, keys = pack(place, tile_cols, tile_counts, x_tiles)
    up, down = send(whole, along_z(4)), send(whole, along_z(-4))
    g1, g3, g2 = send(block, along_x(1)), send(block, along_x(-1)), send(block, along_x(2))
    same, other = sort_panels(place, block, g1, g2, g3, keys)
    far = (send(after(up[:PIECE], other), along_z(4)), send(after(down[PIECE:], other), along_z(-4)))
    r1, rm, r2 = send(other, along_y(1)), send(other, along_y(-1)), send(same, along_y(2))
    left, partner = left_panels(place, same, r1, rm, r2)
    pieces = (whole, up, down, *far)
    near_core, near_halo = edges(True, place, whole, up, down)
    near = (send(near_core, CORE), send(near_halo, HALO))
    far_core, far_halo = edges(False, place, *far)
    received = (send(far_core, CORE), send(far_halo, HALO))
    begun = [begin(BEGIN, h, place, pieces, near, left) for h in range(2)]
    kept, got = [], []
    for h in range(2):
        keep, give = multiply(MULT[h], h, place, received, begun[h], left, keys, partner)
        kept.append(keep)
        got.append(send(give, PLANE))
    return finish(kept[0], got[0], kept[1], got[1])


def solution(mesh):
    placed = (P("row", "col", None, None), P("row", "col"), P("row", "col"))
    return jax.shard_map(
        body, mesh=mesh, in_specs=placed, out_specs=P("row", "col", None, None), check_vma=False
    )
```

```python
import functools

import jax
import jax.numpy as jnp
from jax import lax
from jax.experimental import pallas as pl
from jax.experimental.pallas import tpu as pltpu
from jax.sharding import PartitionSpec as P

BF16, F32, I32 = jnp.bfloat16, jnp.float32, jnp.int32
T = 128
EDGE = (0, 0)
MULT = (3 << 30, 3 << 30)
LEFT = 5600000000
SORT = 0
BEGIN = 0
LIMIT = 48 << 20
BLOCK = 12 * T + 16
HEAD, TAIL = T, T + 16
PIECE = 3 * (HEAD + TAIL)
VMEM = pl.BlockSpec(memory_space=pltpu.VMEM)
SMEM = pl.BlockSpec(memory_space=pltpu.SMEM)


def routes(move):
    pairs = []
    for row in range(64):
        for col in range(8):
            a, z, k, x, h = move(row // 32, row // 2 % 16, row % 2, col // 2, col % 2)
            pairs.append((row * 8 + col, (a * 32 + z % 16 * 2 + k) * 8 + x % 4 * 2 + h))
    return pairs


def along_z(n):
    return routes(lambda a, z, k, x, h: (a, z + n, k, x, h))


def along_x(n):
    return routes(lambda a, z, k, x, h: (a, z, k, x + n, h))


def along_y(n):
    def move(a, z, k, x, h):
        y = (2 * h + a + n) % 4
        return y % 2, z, k, x, y // 2

    return routes(move)


CORE = routes(lambda a, z, k, x, h: (a, z, 1 - k, x, h))
HALO = routes(lambda a, z, k, x, h: (a, z + 2 * k - 1, 1 - k, x, h))
PLANE = routes(lambda a, z, k, x, h: (1 - a, z, k, x, h))


def send(block, pairs):
    return lax.ppermute(block, ("row", "col"), pairs)


def params():
    return pltpu.CompilerParams(vmem_limit_bytes=LIMIT)


def cost(flops, moved):
    return pl.CostEstimate(flops=flops, bytes_accessed=moved, transcendentals=0)


def lanes():
    return lax.broadcasted_iota(I32, (1, T), 1)


def flipped(v):
    return pltpu.roll(v, T // 2, 1)


def chosen(keys, target):
    return jnp.where(keys == target, 1.0, 0.0).astype(BF16)


def turned(v):
    return pltpu.roll(v, T // 2, 1)


def pack_kernel(place, cols, counts, x, a_out, b_out, k_out):
    row = lax.broadcasted_iota(I32, (16, T), 0)
    left = lax.broadcasted_iota(I32, (16, T), 1) < T // 2
    plain = jnp.full((16, T), 9, I32)
    paired = jnp.full((16, T), 9, I32)
    for r in range(3):
        keys = []
        for t in range(4):
            away = (cols[r, t] - (place[0] * 3 + r) + 240) % 24
            away = jnp.where(away > 12, away - 24, away)
            keys.append(jnp.where(t < counts[0, r], away, 9))
            plain = jnp.where(row == r * 4 + t, keys[t], plain)
        for m in range(2):
            first, second = keys[2 * m], keys[2 * m + 1]
            paired = jnp.where(row == r * 4 + 2 * m, jnp.where(left, first, second), paired)
            paired = jnp.where(row == r * 4 + 2 * m + 1, jnp.where(left, second, first), paired)
    a_out[12 * T :, :] = plain.astype(F32).astype(BF16)
    paired = paired.astype(F32)
    k_out[...] = paired.astype(BF16)
    here = lanes() < T // 2
    for r in range(3):
        tail = 3 * HEAD + r * TAIL
        keyed = jnp.concatenate([paired[4 * r : 4 * r + 4], jnp.full((12, T), 9.0, F32)], axis=0)
        keyed = keyed.astype(BF16)
        b_out[tail + T : tail + TAIL, :] = keyed
        b_out[PIECE + tail + T : PIECE + tail + TAIL, :] = keyed
        for m in range(2):
            at = r * HEAD if m == 0 else tail
            even = x[r, 2 * m]
            odd = x[r, 2 * m + 1]
            a_out[(4 * r + 2 * m) * T : (4 * r + 2 * m + 1) * T, :] = even
            a_out[(4 * r + 2 * m + 1) * T : (4 * r + 2 * m + 2) * T, :] = odd
            even, odd = even.astype(F32), odd.astype(F32)
            b_out[at : at + T, :] = jnp.where(here, even, turned(odd)).astype(BF16)
            b_out[PIECE + at : PIECE + at + T, :] = jnp.where(here, turned(even), odd).astype(BF16)


def pack(place, cols, counts, x):
    shapes = ((BLOCK, T), (2 * PIECE, T), (16, T))
    return pl.pallas_call(
        pack_kernel,
        out_shape=[jax.ShapeDtypeStruct(s, BF16) for s in shapes],
        in_specs=[SMEM, SMEM, SMEM, VMEM],
        out_specs=[VMEM] * 3,
        compiler_params=params(),
        cost_estimate=cost(1 << 20, 6 << 20),
        name="pack",
    )(place, cols, counts.T, x)


def sort_kernel(place, own, g1, g2, g3, keys, same, other):
    a, x = place[1], place[4]
    other[2 * BLOCK :, :] = keys[...]
    for k, source in enumerate((own, g1, g2, g3)):
        panel = (x - k + 4) % 4
        at = pl.multiple_of(panel % 2 * BLOCK, 16)

        @pl.when(panel // 2 == a)
        def _(source=source, at=at):
            same[pl.ds(at, BLOCK), :] = source[...]

        @pl.when(panel // 2 != a)
        def _(source=source, at=at):
            other[pl.ds(at, BLOCK), :] = source[...]


def sort_panels(place, own, g1, g2, g3, keys):
    return pl.pallas_call(
        sort_kernel,
        out_shape=[
            jax.ShapeDtypeStruct((2 * BLOCK, T), BF16),
            jax.ShapeDtypeStruct((2 * BLOCK + 16, T), BF16),
        ],
        in_specs=[SMEM] + [VMEM] * 5,
        out_specs=[VMEM] * 2,
        compiler_params=params(),
        cost_estimate=cost(SORT, 4 << 20),
        name="sort_panels",
    )(place, own, g1, g2, g3, keys)


def left_kernel(place, same, r1, rm, r2, out, partner):
    a, h = place[1], place[5]
    near = jnp.where(a == 1, h, 1 - h)
    keys = slice(2 * BLOCK, 2 * BLOCK + 16)
    partner[...] = jnp.where(a == 1, r1[keys, :].astype(F32), rm[keys, :].astype(F32)).astype(BF16)
    for n, (source, half) in enumerate(((same, h), (r2, 1 - h), (r1, near), (rm, 1 - near))):
        rows = slice(n // 2 * T, (n // 2 + 1) * T)

        def one(e, carry, source=source, half=half, rows=rows):
            base = pl.multiple_of(e * BLOCK, 16)
            keys = source[pl.ds(base + 12 * T, 16), :].astype(F32)
            for i in range(3):
                tiles = [source[pl.ds(base + (4 * i + t) * T, T), :] for t in range(4)]
                for d in range(5):
                    parts = [tiles[t] * chosen(keys[4 * i + t : 4 * i + t + 1], float(d - 2)) for t in range(4)]
                    block = (parts[0] + parts[1]) + (parts[2] + parts[3])
                    out[i, 2 * e + half, rows, d * T : (d + 1) * T] = block
            return carry

        lax.fori_loop(0, 2, one, 0)


def left_panels(place, same, r1, rm, r2):
    return pl.pallas_call(
        left_kernel,
        out_shape=[
            jax.ShapeDtypeStruct((3, 4, 2 * T, 5 * T), BF16),
            jax.ShapeDtypeStruct((16, T), BF16),
        ],
        in_specs=[SMEM] + [VMEM] * 4,
        out_specs=[VMEM, VMEM],
        compiler_params=params(),
        cost_estimate=cost(LEFT, 8 << 20),
        name="left_panels",
    )(place, same, r1, rm, r2)


EDGE_ROWS = 2 * (HEAD + TAIL)


def edge_kernel(place, own, up, down, far0, far1, to_core, to_halo):
    b, core = place[2], place[3]
    for out, start in ((to_core, 1 - core), (to_halo, core)):
        for source, panel in ((own, b), (up, (b + 3) % 4), (down, (b + 1) % 4), (None, (b + 2) % 4)):
            for h in range(2):
                held = (far0, far1)[h] if source is None else source
                base = 0 if source is None else h * PIECE
                for first, size, into in ((0, HEAD, 0), (3 * HEAD, TAIL, 2 * HEAD)):
                    begin = pl.multiple_of(base + first + start * size, 16)
                    out[h, panel, into : into + 2 * size, :] = held[pl.ds(begin, 2 * size), :]


def edges(flops, place, *sources):
    shape = jax.ShapeDtypeStruct((2, 4, EDGE_ROWS, T), BF16)
    return pl.pallas_call(
        edge_kernel,
        out_shape=[shape, shape],
        in_specs=[SMEM] + [VMEM] * 5,
        out_specs=[VMEM] * 2,
        compiler_params=params(),
        cost_estimate=cost(flops, 4 << 20),
        name="edges",
    )(place, *sources)


def place_row(k, v0, v1, keys, right, at, row, clear):
    half = (lanes() >= T // 2).astype(F32)
    keys = keys.astype(F32) + float(k)
    w0, w1 = flipped(v0), flipped(v1)
    for w in range(4):
        into = (at, slice(row * T, (row + 1) * T), slice(w * T, (w + 1) * T))
        if 2 * w + 1 < k - 2 or 2 * w > k + 2:
            if clear:
                right[into] = jnp.zeros((T, T), BF16)
            continue
        pick = [chosen(keys[n : n + 1], half + float(2 * w)) for n in range(4)]
        right[into] = (v0 * pick[0] + w0 * pick[1]) + (v1 * pick[2] + w1 * pick[3])


def begin_kernel(h, place, own, up, down, far0, far1, left, out, right):
    sums = [None] * 3
    for p, (source, shift) in enumerate(((own, 0), (up, 3), (down, 1), (None, 2))):
        panel = (place[2] + shift) % 4
        held = (far0, far1)[h] if source is None else source
        base = 0 if source is None else h * PIECE
        for r in range(3):
            head = base + r * HEAD
            tail = base + 3 * HEAD + r * TAIL
            keys = held[tail + T : tail + TAIL, :]
            place_row(r + 2, held[head : head + T, :], held[tail : tail + T, :], keys, right, p % 2, r, p < 2)
        for i in range(3):
            first = i // 2 * T
            part = jnp.dot(
                left[i, panel, :, (2 - i) * T : (5 - i) * T],
                right[p % 2, :, first : first + 3 * T],
                preferred_element_type=F32,
            )
            sums[i] = part if sums[i] is None else sums[i] + part
    for i in range(3):
        out[i] = sums[i]


def begin(flops, h, place, pieces, left):
    return pl.pallas_call(
        functools.partial(begin_kernel, h),
        out_shape=jax.ShapeDtypeStruct((3, 2 * T, 3 * T), F32),
        in_specs=[SMEM] + [VMEM] * 6,
        out_specs=VMEM,
        scratch_shapes=[pltpu.VMEM((2, 3 * T, 4 * T), BF16)],
        compiler_params=params(),
        cost_estimate=cost(flops, 6 << 20),
        name="begin",
    )(place, *pieces, left)


def multiply_kernel(h, place, from_core, from_halo, begun, left, mine, partner, keep, give, right):
    b, core = place[2], place[3]
    half = (lanes() >= T // 2).astype(F32)
    sums = [begun[i] for i in range(3)]
    for panel in range(4):

        def edge(first, size, low, panel=panel):
            rows = slice(first, first + size)
            above, below = (from_halo, from_core) if low else (from_core, from_halo)
            return jnp.where(core == 0, above[h, panel, rows, :], below[h, panel, rows, :])

        for n, k in enumerate((0, 1, 5, 6)):
            row, low = n % 2, n < 2
            tail = 2 * HEAD + row * TAIL
            keys = edge(tail + T, 16, low)
            place_row(k, edge(row * HEAD, T, low), edge(tail, T, low), keys, right, panel % 2, n, panel < 2)
        for i in range(3):
            first = i // 2 * T
            side = left[i, panel]
            if i == 1:
                side = jnp.concatenate([side[:, :T], side[:, 4 * T :]], axis=1)
            else:
                side = side[:, : 2 * T] if i == 0 else side[:, 3 * T :]
            sums[i] = sums[i] + jnp.dot(
                side,
                right[panel % 2, i * T : (i + 2) * T, first : first + 3 * T],
                preferred_element_type=F32,
            )
    for i in range(3):
        for side, (out, source) in enumerate(((keep, mine), (give, partner))):
            keys = source[...].astype(F32)[4 * i : 4 * i + 4] + float(i + 2)
            for m in range(2):
                total = None
                for w in range(3):
                    v = sums[i][side * T : (side + 1) * T, w * T : (w + 1) * T]
                    target = half + float(2 * (w + i // 2))
                    swap = (1.0 - half) + float(2 * (w + i // 2))
                    key = keys[2 * m : 2 * m + 1]
                    part = v * jnp.where(key == target, 1.0, 0.0)
                    part = part + turned(v) * jnp.where(key == swap, 1.0, 0.0)
                    total = part if total is None else total + part
                out[i, m] = total


def multiply(flops, h, place, received, begun, left, mine, partner):
    shape = jax.ShapeDtypeStruct((3, 2, T, T), F32)
    return pl.pallas_call(
        functools.partial(multiply_kernel, h),
        out_shape=[shape, shape],
        in_specs=[SMEM] + [VMEM] * 6,
        out_specs=[VMEM, VMEM],
        scratch_shapes=[pltpu.VMEM((2, 4 * T, 4 * T), BF16)],
        compiler_params=params(),
        cost_estimate=cost(flops, 10 << 20),
        name="multiply",
    )(place, *received, begun, left, mine, partner)


def finish_kernel(own0, got0, own1, got1, out):
    here = lanes() < T // 2
    for i in range(3):
        for m in range(2):
            low = own0[i, m] + got0[i, m]
            high = own1[i, m] + got1[i, m]
            out[i, 2 * m] = jnp.where(here, low, turned(high)).astype(BF16)
            out[i, 2 * m + 1] = jnp.where(here, turned(low), high).astype(BF16)


def finish(own0, got0, own1, got1):
    return pl.pallas_call(
        finish_kernel,
        out_shape=jax.ShapeDtypeStruct((3, 4, T, T), BF16),
        in_specs=[VMEM] * 4,
        out_specs=VMEM,
        compiler_params=params(),
        cost_estimate=cost(1 << 20, 2 << 20),
        name="finish",
    )(own0, got0, own1, got1)


def after(value, *others):
    return lax.optimization_barrier((value,) + others)[0]


def body(x_tiles, tile_cols, tile_counts):
    row, col = lax.axis_index("row"), lax.axis_index("col")
    place = jnp.stack([row, row // 32, row // 8 % 4, row % 2, col // 2, col % 2]).astype(I32)
    block, whole, keys = pack(place, tile_cols, tile_counts, x_tiles)
    up, down = send(whole, along_z(4)), send(whole, along_z(-4))
    g1, g3, g2 = send(block, along_x(1)), send(block, along_x(-1)), send(block, along_x(2))
    same, other = sort_panels(place, block, g1, g2, g3, keys)
    far = (send(after(up[:PIECE], other), along_z(4)), send(after(down[PIECE:], other), along_z(-4)))
    r1, rm, r2 = send(other, along_y(1)), send(other, along_y(-1)), send(same, along_y(2))
    left, partner = left_panels(place, same, r1, rm, r2)
    pieces = (whole, up, down, *far)
    to_core, to_halo = edges(EDGE[0], place, *pieces)
    received = (send(to_core, CORE), send(to_halo, HALO))
    begun = [begin(BEGIN, h, place, pieces, left) for h in range(2)]
    kept, got = [], []
    for h in range(2):
        keep, give = multiply(MULT[h], h, place, received, begun[h], left, keys, partner)
        kept.append(keep)
        got.append(send(give, PLANE))
    return finish(kept[0], got[0], kept[1], got[1])


def solution(mesh):
    placed = (P("row", "col", None, None), P("row", "col"), P("row", "col"))
    return jax.shard_map(
        body, mesh=mesh, in_specs=placed, out_specs=P("row", "col", None, None), check_vma=False
    )
```

```python
import functools

import jax
import jax.numpy as jnp
from jax import lax
from jax.experimental import pallas as pl
from jax.experimental.pallas import tpu as pltpu
from jax.sharding import PartitionSpec as P

BF16, F32, I32 = jnp.bfloat16, jnp.float32, jnp.int32
T = 128
EDGE = (0, 0)
MULT = (3 << 30, 3 << 30)
LEFT = 5600000000
SORT = 0
BEGIN = 0
LIMIT = 48 << 20
BLOCK = 12 * T + 16
HEAD, TAIL = T, T + 16
PIECE = 3 * (HEAD + TAIL)
VMEM = pl.BlockSpec(memory_space=pltpu.VMEM)
SMEM = pl.BlockSpec(memory_space=pltpu.SMEM)


def routes(move):
    pairs = []
    for row in range(64):
        for col in range(8):
            a, z, k, x, h = move(row // 32, row // 2 % 16, row % 2, col // 2, col % 2)
            pairs.append((row * 8 + col, (a * 32 + z % 16 * 2 + k) * 8 + x % 4 * 2 + h))
    return pairs


def along_z(n):
    return routes(lambda a, z, k, x, h: (a, z + n, k, x, h))


def along_x(n):
    return routes(lambda a, z, k, x, h: (a, z, k, x + n, h))


def along_y(n):
    def move(a, z, k, x, h):
        y = (2 * h + a + n) % 4
        return y % 2, z, k, x, y // 2

    return routes(move)


CORE = routes(lambda a, z, k, x, h: (a, z, 1 - k, x, h))
HALO = routes(lambda a, z, k, x, h: (a, z + 2 * k - 1, 1 - k, x, h))
PLANE = routes(lambda a, z, k, x, h: (1 - a, z, k, x, h))


def send(block, pairs):
    return lax.ppermute(block, ("row", "col"), pairs)


def params():
    return pltpu.CompilerParams(vmem_limit_bytes=LIMIT)


def cost(flops, moved):
    return pl.CostEstimate(flops=flops, bytes_accessed=moved, transcendentals=0)


def lanes():
    return lax.broadcasted_iota(I32, (1, T), 1)


def flipped(v):
    return pltpu.roll(v, T // 2, 1)


def chosen(keys, target):
    return jnp.where(keys == target, 1.0, 0.0).astype(BF16)


def turned(v):
    return pltpu.roll(v, T // 2, 1)


def pack_kernel(place, x, a_out, b_out, k_out):
    row = lax.broadcasted_iota(I32, (16, T), 0)
    left = lax.broadcasted_iota(I32, (16, T), 1) < T // 2
    plain = jnp.full((16, T), 9, I32)
    paired = jnp.full((16, T), 9, I32)
    for r in range(3):
        keys = []
        for t in range(4):
            away = (place[6 + 4 * r + t] - (place[0] * 3 + r) + 240) % 24
            away = jnp.where(away > 12, away - 24, away)
            keys.append(jnp.where(t < place[18 + r], away, 9))
            plain = jnp.where(row == r * 4 + t, keys[t], plain)
        for m in range(2):
            first, second = keys[2 * m], keys[2 * m + 1]
            paired = jnp.where(row == r * 4 + 2 * m, jnp.where(left, first, second), paired)
            paired = jnp.where(row == r * 4 + 2 * m + 1, jnp.where(left, second, first), paired)
    a_out[12 * T :, :] = plain.astype(F32).astype(BF16)
    paired = paired.astype(F32)
    k_out[...] = paired.astype(BF16)
    here = lanes() < T // 2
    for r in range(3):
        tail = 3 * HEAD + r * TAIL
        keyed = jnp.concatenate([paired[4 * r : 4 * r + 4], jnp.full((12, T), 9.0, F32)], axis=0)
        keyed = keyed.astype(BF16)
        b_out[tail + T : tail + TAIL, :] = keyed
        b_out[PIECE + tail + T : PIECE + tail + TAIL, :] = keyed
        for m in range(2):
            at = r * HEAD if m == 0 else tail
            even = x[r, 2 * m]
            odd = x[r, 2 * m + 1]
            a_out[(4 * r + 2 * m) * T : (4 * r + 2 * m + 1) * T, :] = even
            a_out[(4 * r + 2 * m + 1) * T : (4 * r + 2 * m + 2) * T, :] = odd
            even, odd = even.astype(F32), odd.astype(F32)
            b_out[at : at + T, :] = jnp.where(here, even, turned(odd)).astype(BF16)
            b_out[PIECE + at : PIECE + at + T, :] = jnp.where(here, turned(even), odd).astype(BF16)


def pack(place, x):
    shapes = ((BLOCK, T), (2 * PIECE, T), (16, T))
    return pl.pallas_call(
        pack_kernel,
        out_shape=[jax.ShapeDtypeStruct(s, BF16) for s in shapes],
        in_specs=[SMEM, VMEM],
        out_specs=[VMEM] * 3,
        compiler_params=params(),
        cost_estimate=cost(1 << 20, 6 << 20),
        name="pack",
    )(place, x)


def sort_kernel(place, own, g1, g2, g3, keys, same, other):
    a, x = place[1], place[4]
    other[2 * BLOCK :, :] = keys[...]
    for k, source in enumerate((own, g1, g2, g3)):
        panel = (x - k + 4) % 4
        at = pl.multiple_of(panel % 2 * BLOCK, 16)

        @pl.when(panel // 2 == a)
        def _(source=source, at=at):
            same[pl.ds(at, BLOCK), :] = source[...]

        @pl.when(panel // 2 != a)
        def _(source=source, at=at):
            other[pl.ds(at, BLOCK), :] = source[...]


def sort_panels(place, own, g1, g2, g3, keys):
    return pl.pallas_call(
        sort_kernel,
        out_shape=[
            jax.ShapeDtypeStruct((2 * BLOCK, T), BF16),
            jax.ShapeDtypeStruct((2 * BLOCK + 16, T), BF16),
        ],
        in_specs=[SMEM] + [VMEM] * 5,
        out_specs=[VMEM] * 2,
        compiler_params=params(),
        cost_estimate=cost(SORT, 4 << 20),
        name="sort_panels",
    )(place, own, g1, g2, g3, keys)


def left_kernel(place, same, r1, rm, r2, out, partner):
    a, h = place[1], place[5]
    near = jnp.where(a == 1, h, 1 - h)
    keys = slice(2 * BLOCK, 2 * BLOCK + 16)
    partner[...] = jnp.where(a == 1, r1[keys, :].astype(F32), rm[keys, :].astype(F32)).astype(BF16)
    for n, (source, half) in enumerate(((same, h), (r2, 1 - h), (r1, near), (rm, 1 - near))):
        rows = slice(n // 2 * T, (n // 2 + 1) * T)

        def one(e, carry, source=source, half=half, rows=rows):
            base = pl.multiple_of(e * BLOCK, 16)
            keys = source[pl.ds(base + 12 * T, 16), :].astype(F32)
            for i in range(3):
                tiles = [source[pl.ds(base + (4 * i + t) * T, T), :] for t in range(4)]
                for d in range(5):
                    parts = [tiles[t] * chosen(keys[4 * i + t : 4 * i + t + 1], float(d - 2)) for t in range(4)]
                    block = (parts[0] + parts[1]) + (parts[2] + parts[3])
                    out[i, 2 * e + half, rows, d * T : (d + 1) * T] = block
            return carry

        lax.fori_loop(0, 2, one, 0)


def left_panels(place, same, r1, rm, r2):
    return pl.pallas_call(
        left_kernel,
        out_shape=[
            jax.ShapeDtypeStruct((3, 4, 2 * T, 5 * T), BF16),
            jax.ShapeDtypeStruct((16, T), BF16),
        ],
        in_specs=[SMEM] + [VMEM] * 4,
        out_specs=[VMEM, VMEM],
        compiler_params=params(),
        cost_estimate=cost(LEFT, 8 << 20),
        name="left_panels",
    )(place, same, r1, rm, r2)


EDGE_ROWS = 2 * (HEAD + TAIL)


def edge_kernel(place, own, up, down, far0, far1, to_core, to_halo):
    b, core = place[2], place[3]
    for out, start in ((to_core, 1 - core), (to_halo, core)):
        for source, panel in ((own, b), (up, (b + 3) % 4), (down, (b + 1) % 4), (None, (b + 2) % 4)):
            for h in range(2):
                held = (far0, far1)[h] if source is None else source
                base = 0 if source is None else h * PIECE
                for first, size, into in ((0, HEAD, 0), (3 * HEAD, TAIL, 2 * HEAD)):
                    begin = pl.multiple_of(base + first + start * size, 16)
                    out[h, panel, into : into + 2 * size, :] = held[pl.ds(begin, 2 * size), :]


def edges(flops, place, *sources):
    shape = jax.ShapeDtypeStruct((2, 4, EDGE_ROWS, T), BF16)
    return pl.pallas_call(
        edge_kernel,
        out_shape=[shape, shape],
        in_specs=[SMEM] + [VMEM] * 5,
        out_specs=[VMEM] * 2,
        compiler_params=params(),
        cost_estimate=cost(flops, 4 << 20),
        name="edges",
    )(place, *sources)


def place_row(k, v0, v1, keys, right, at, row, clear):
    half = (lanes() >= T // 2).astype(F32)
    keys = keys.astype(F32) + float(k)
    w0, w1 = flipped(v0), flipped(v1)
    for w in range(4):
        into = (at, slice(row * T, (row + 1) * T), slice(w * T, (w + 1) * T))
        if 2 * w + 1 < k - 2 or 2 * w > k + 2:
            if clear:
                right[into] = jnp.zeros((T, T), BF16)
            continue
        pick = [chosen(keys[n : n + 1], half + float(2 * w)) for n in range(4)]
        right[into] = (v0 * pick[0] + w0 * pick[1]) + (v1 * pick[2] + w1 * pick[3])


def begin_kernel(h, place, own, up, down, far0, far1, left, out, right):
    sums = [None] * 3
    for p, (source, shift) in enumerate(((own, 0), (up, 3), (down, 1), (None, 2))):
        panel = (place[2] + shift) % 4
        held = (far0, far1)[h] if source is None else source
        base = 0 if source is None else h * PIECE
        for r in range(3):
            head = base + r * HEAD
            tail = base + 3 * HEAD + r * TAIL
            keys = held[tail + T : tail + TAIL, :]
            place_row(r + 2, held[head : head + T, :], held[tail : tail + T, :], keys, right, p % 2, r, p < 2)
        for i in range(3):
            first = i // 2 * T
            part = jnp.dot(
                left[i, panel, :, (2 - i) * T : (5 - i) * T],
                right[p % 2, :, first : first + 3 * T],
                preferred_element_type=F32,
            )
            sums[i] = part if sums[i] is None else sums[i] + part
    for i in range(3):
        out[i] = sums[i]


def begin(flops, h, place, pieces, left):
    return pl.pallas_call(
        functools.partial(begin_kernel, h),
        out_shape=jax.ShapeDtypeStruct((3, 2 * T, 3 * T), F32),
        in_specs=[SMEM] + [VMEM] * 6,
        out_specs=VMEM,
        scratch_shapes=[pltpu.VMEM((2, 3 * T, 4 * T), BF16)],
        compiler_params=params(),
        cost_estimate=cost(flops, 6 << 20),
        name="begin",
    )(place, *pieces, left)


def multiply_kernel(h, place, from_core, from_halo, begun, left, mine, partner, keep, give, right):
    b, core = place[2], place[3]
    half = (lanes() >= T // 2).astype(F32)
    sums = [begun[i] for i in range(3)]
    for panel in range(4):

        def edge(first, size, low, panel=panel):
            rows = slice(first, first + size)
            above, below = (from_halo, from_core) if low else (from_core, from_halo)
            return jnp.where(core == 0, above[h, panel, rows, :], below[h, panel, rows, :])

        for n, k in enumerate((0, 1, 5, 6)):
            row, low = n % 2, n < 2
            tail = 2 * HEAD + row * TAIL
            keys = edge(tail + T, 16, low)
            place_row(k, edge(row * HEAD, T, low), edge(tail, T, low), keys, right, panel % 2, n, panel < 2)
        for i in range(3):
            first = i // 2 * T
            side = left[i, panel]
            if i == 1:
                side = jnp.concatenate([side[:, :T], side[:, 4 * T :]], axis=1)
            else:
                side = side[:, : 2 * T] if i == 0 else side[:, 3 * T :]
            sums[i] = sums[i] + jnp.dot(
                side,
                right[panel % 2, i * T : (i + 2) * T, first : first + 3 * T],
                preferred_element_type=F32,
            )
    for i in range(3):
        for side, (out, source) in enumerate(((keep, mine), (give, partner))):
            keys = source[...].astype(F32)[4 * i : 4 * i + 4] + float(i + 2)
            for m in range(2):
                total = None
                for w in range(3):
                    v = sums[i][side * T : (side + 1) * T, w * T : (w + 1) * T]
                    target = half + float(2 * (w + i // 2))
                    swap = (1.0 - half) + float(2 * (w + i // 2))
                    key = keys[2 * m : 2 * m + 1]
                    part = v * jnp.where(key == target, 1.0, 0.0)
                    part = part + turned(v) * jnp.where(key == swap, 1.0, 0.0)
                    total = part if total is None else total + part
                out[i, m] = total


def multiply(flops, h, place, received, begun, left, mine, partner):
    shape = jax.ShapeDtypeStruct((3, 2, T, T), F32)
    return pl.pallas_call(
        functools.partial(multiply_kernel, h),
        out_shape=[shape, shape],
        in_specs=[SMEM] + [VMEM] * 6,
        out_specs=[VMEM, VMEM],
        scratch_shapes=[pltpu.VMEM((2, 4 * T, 4 * T), BF16)],
        compiler_params=params(),
        cost_estimate=cost(flops, 10 << 20),
        name="multiply",
    )(place, *received, begun, left, mine, partner)


def finish_kernel(own0, got0, own1, got1, out):
    here = lanes() < T // 2
    for i in range(3):
        for m in range(2):
            low = own0[i, m] + got0[i, m]
            high = own1[i, m] + got1[i, m]
            out[i, 2 * m] = jnp.where(here, low, turned(high)).astype(BF16)
            out[i, 2 * m + 1] = jnp.where(here, turned(low), high).astype(BF16)


def finish(own0, got0, own1, got1):
    return pl.pallas_call(
        finish_kernel,
        out_shape=jax.ShapeDtypeStruct((3, 4, T, T), BF16),
        in_specs=[VMEM] * 4,
        out_specs=VMEM,
        compiler_params=params(),
        cost_estimate=cost(1 << 20, 2 << 20),
        name="finish",
    )(own0, got0, own1, got1)


def after(value, *others):
    return lax.optimization_barrier((value,) + others)[0]


def body(x_tiles, tile_cols, tile_counts):
    row, col = lax.axis_index("row"), lax.axis_index("col")
    place = jnp.stack([row, row // 32, row // 8 % 4, row % 2, col // 2, col % 2]).astype(I32)
    place = jnp.concatenate([place, tile_cols.reshape(12), tile_counts.reshape(3)])
    block, whole, keys = pack(place, x_tiles)
    up, down = send(whole, along_z(4)), send(whole, along_z(-4))
    g1, g3, g2 = send(block, along_x(1)), send(block, along_x(-1)), send(block, along_x(2))
    same, other = sort_panels(place, block, g1, g2, g3, keys)
    far = (send(after(up[:PIECE], other), along_z(4)), send(after(down[PIECE:], other), along_z(-4)))
    r1, rm, r2 = send(other, along_y(1)), send(other, along_y(-1)), send(same, along_y(2))
    left, partner = left_panels(place, same, r1, rm, r2)
    pieces = (whole, up, down, *far)
    to_core, to_halo = edges(EDGE[0], place, *pieces)
    received = (send(to_core, CORE), send(to_halo, HALO))
    begun = [begin(BEGIN, h, place, pieces, left) for h in range(2)]
    kept, got = [], []
    for h in range(2):
        keep, give = multiply(MULT[h], h, place, received, begun[h], left, keys, partner)
        kept.append(keep)
        got.append(send(give, PLANE))
    return finish(kept[0], got[0], kept[1], got[1])


def solution(mesh):
    placed = (P("row", "col", None, None), P("row", "col"), P("row", "col"))
    return jax.shard_map(
        body, mesh=mesh, in_specs=placed, out_specs=P("row", "col", None, None), check_vma=False
    )
```
